32 devices in a mesh: dp: 16 (over z, x, core), blk: 2 (over y).
Axes of the slice: x: 2, y: 2, z: 4, core: 2. Of those that a mesh axis runs over, the one named last changes fastest.
Arguments:
- patches: bfloat16 [16, 1280, 768], P('dp', 'blk'), may hold values from -6 to 6
- segments: int32 [16, 1280], P('dp'), may hold values from 0 to 7, as said below
- cotangent: bfloat16 [16, 1280, 768], P('dp', 'blk'), may hold values from -6 to 6
- qkv_weight: float32 [768, 2304], P(('dp', 'blk')), may hold values from -0.21875 to 0.21875
- out_weight: float32 [768, 768], P(('dp', 'blk')), may hold values from -0.875 to 0.875
- in_weight: float32 [768, 3072], P(('dp', 'blk')), may hold values from -0.21875 to 0.21875
- back_weight: float32 [3072, 768], P(('dp', 'blk')), may hold values from -0.109375 to 0.109375
- norm_gains: float32 [768, 4], P(('dp', 'blk')), may hold values from 0.1 to 1.9
- qkv_first: float32 [768, 2304], P(('dp', 'blk')), may hold values from -181.01933 to 181.01933
- out_first: float32 [768, 768], P(('dp', 'blk')), may hold values from -70.10849 to 70.10849
- in_first: float32 [768, 3072], P(('dp', 'blk')), may hold values from -198.29675 to 198.29675
- back_first: float32 [3072, 768], P(('dp', 'blk')), may hold values from -362.03867 to 362.03867
- gain_first: float32 [768, 4], P(('dp', 'blk')), may hold values from -404.77155 to 404.77155
- qkv_second: float32 [768, 2304], P(('dp', 'blk')), may hold values from 1024 to 8192
- out_second: float32 [768, 768], P(('dp', 'blk')), may hold values from 153.6 to 1228.8
- in_second: float32 [768, 3072], P(('dp', 'blk')), may hold values from 1228.8 to 9830.4
- back_second: float32 [3072, 768], P(('dp', 'blk')), may hold values from 4096 to 32768
- gain_second: float32 [768, 4], P(('dp', 'blk')), may hold values from 5120 to 40960
Outputs:
- block_out: bfloat16 [16, 1280, 768], P('dp', 'blk')
- patch_grad: bfloat16 [16, 1280, 768], P('dp', 'blk')
- qkv_moment: float32 [768, 2304], P(('dp', 'blk'))
- qkv_square: float32 [768, 2304], P(('dp', 'blk'))
- qkv_new: float32 [768, 2304], P(('dp', 'blk'))
- out_moment: float32 [768, 768], P(('dp', 'blk'))
- out_square: float32 [768, 768], P(('dp', 'blk'))
- out_new: float32 [768, 768], P(('dp', 'blk'))
- in_moment: float32 [768, 3072], P(('dp', 'blk'))
- in_square: float32 [768, 3072], P(('dp', 'blk'))
- in_new: float32 [768, 3072], P(('dp', 'blk'))
- back_moment: float32 [3072, 768], P(('dp', 'blk'))
- back_square: float32 [3072, 768], P(('dp', 'blk'))
- back_new: float32 [3072, 768], P(('dp', 'blk'))
- gain_moment: float32 [768, 4], P(('dp', 'blk'))
- gain_square: float32 [768, 4], P(('dp', 'blk'))
- gain_new: float32 [768, 4], P(('dp', 'blk'))
The draws below stay inside these ranges and needn't reach their ends.
Inputs may be any that keep to these rules, and one draw needn't show every extreme that they name: `segments`: in each group, positions 0 to 1023 hold the long sequence: images 0, 1 and 2 in order, image 1 of exactly 576 patches, then one or more padding patches (7); the remaining positions hold the short sequence: images 3, 4, 5 and 6 in order, each of a quarter of 64 to 63 patches, then padding (7).
All inputs are finite; a program needn't handle non-finite values.
Results may differ from the reference program's by a relative error of at most 0.012.
The reference program's roundings to bfloat16 on the way count: a program that leaves them out, or rounds other values in their place, can miss the bound.
Values may be sent and summed in bfloat16 or wider, within the bound.
A program may use at most 192 MiB of HBM per device.

```python
import math
import jax
import jax.numpy as jnp
from jax import lax

D = 768
H = 12
FF = 3072
HD = 64
LONG_LEN = 1024
SHORT_LEN = 256
BIG_IMG = 576
SMALL_IMG = 64
STEP = 5
ROW = 1280
GROUPS = 16
TOKENS = 20480


pad_mark = 7


def segment_row(key):
    half_row = (LONG_LEN + SHORT_LEN) // 2
    first_lo = max(1, half_row - BIG_IMG + 1)
    first_hi = min(half_row - 1, LONG_LEN - BIG_IMG - 2)
    key_first, key_third, key_short = jax.random.split(key, 3)
    first_len = jax.random.randint(key_first, (), first_lo, first_hi + 1).astype(jnp.int32)
    rest_len = LONG_LEN - BIG_IMG - first_len
    third_len = jax.random.randint(key_third, (), 1, rest_len).astype(jnp.int32)
    long_pos = jnp.arange(LONG_LEN, dtype=jnp.int32)
    long_ids = (long_pos >= first_len).astype(jnp.int32) + (long_pos >= first_len + BIG_IMG).astype(jnp.int32) + (long_pos >= first_len + BIG_IMG + third_len).astype(jnp.int32)
    long_ids = jnp.where(long_ids == 3, pad_mark, long_ids).astype(jnp.int32)
    image_sizes = jax.random.randint(key_short, (4,), max(1, SMALL_IMG // 4), SMALL_IMG).astype(jnp.int32)
    image_ends = jnp.cumsum(image_sizes).astype(jnp.int32)
    short_pos = jnp.arange(SHORT_LEN, dtype=jnp.int32)
    passed = jnp.sum((short_pos[:, None] >= image_ends[None, :]).astype(jnp.int32), axis=1)
    short_ids = jnp.where(passed == 4, pad_mark, 3 + passed).astype(jnp.int32)
    return jnp.concatenate([long_ids, short_ids]).astype(jnp.int32)


def draw_segments(key, part):
    key = jax.random.fold_in(key, 11)
    subkeys = jax.random.split(key, GROUPS)
    return jax.vmap(segment_row)(subkeys).astype(jnp.int32)


def block_scale(rng, shape, cuts, least, largest):
    level, own = 1.0, jax.random.fold_in(rng, 6)
    for axis_at, shards_of in cuts:
        steps = jnp.exp(jax.random.uniform(jax.random.fold_in(own, axis_at), (shards_of,), jnp.float32, least / len(cuts), largest / len(cuts)))
        level = level * jnp.repeat(steps, shape[axis_at] // shards_of).reshape([-1 if axis == axis_at else 1 for axis in range(len(shape))])
    return level


def noise(own_key, dims, width, limit, cuts=(), kind=jnp.bfloat16):
    entries = width * jax.random.normal(own_key, dims, jnp.float32)
    if cuts:
        entries = entries * block_scale(own_key, dims, cuts, -0.22, 0.18)
    return jnp.clip(entries, -limit, limit).astype(kind)


def setup_inputs(seed: int = 0) -> dict:
    arg_keys = jax.random.split(jax.random.key(seed), 19)
    patches = noise(arg_keys[0], (GROUPS, ROW, D), 1.0, 6.0, ((0, 16), (1, 2)))
    segments = draw_segments(jax.random.fold_in(arg_keys[18], 71), 0)
    cotangent = noise(arg_keys[2], (GROUPS, ROW, D), 1.0, 6.0, ((0, 16), (1, 2)))
    qkv_weight = noise(arg_keys[3], (D, 3 * D), D ** -0.5, 0.21875, ((0, 32),), jnp.float32)
    out_weight = noise(arg_keys[4], (D, D), (D // 16) ** -0.5, 0.875, ((0, 32),), jnp.float32)
    in_weight = noise(arg_keys[5], (D, FF), D ** -0.5, 0.21875, ((0, 32),), jnp.float32)
    back_weight = noise(arg_keys[6], (FF, D), FF ** -0.5, 0.109375, ((0, 32),), jnp.float32)
    norm_gains = jnp.clip(1.0 + 0.18 * jax.random.normal(arg_keys[7], (D, 4), jnp.float32), 0.1, 1.9)
    qkv_first = noise(arg_keys[8], (D, 3 * D), ((0.1 * TOKENS) ** 0.5), 181.01933, ((0, 32),), jnp.float32)
    out_first = noise(arg_keys[9], (D, D), ((0.015 * TOKENS) ** 0.5), 70.10849, ((0, 32),), jnp.float32)
    in_first = noise(arg_keys[10], (D, FF), ((0.12 * TOKENS) ** 0.5), 198.29675, ((0, 32),), jnp.float32)
    back_first = noise(arg_keys[11], (FF, D), ((0.4 * TOKENS) ** 0.5), 362.03867, ((0, 32),), jnp.float32)
    gain_first = noise(arg_keys[12], (D, 4), ((0.5 * TOKENS) ** 0.5), 404.77155, ((0, 32),), jnp.float32)
    qkv_second = jnp.clip(jnp.exp(math.log(8192.0) - 2.0794415 * jax.random.uniform(arg_keys[13], (D, 3 * D), jnp.float32) ** block_scale(arg_keys[13], (D, 3 * D), ((0, 32),), -0.2, 0.2)), 1024.0, 8192.0)
    out_second = jnp.clip(jnp.exp(math.log(1228.8) - 2.0794415 * jax.random.uniform(arg_keys[14], (D, D), jnp.float32) ** block_scale(arg_keys[14], (D, D), ((0, 32),), -0.2, 0.2)), 153.6, 1228.8)
    in_second = jnp.clip(jnp.exp(math.log(9830.4) - 2.0794415 * jax.random.uniform(arg_keys[15], (D, FF), jnp.float32) ** block_scale(arg_keys[15], (D, FF), ((0, 32),), -0.2, 0.2)), 1228.8, 9830.4)
    back_second = jnp.clip(jnp.exp(math.log(32768.0) - 2.0794415 * jax.random.uniform(arg_keys[16], (FF, D), jnp.float32) ** block_scale(arg_keys[16], (FF, D), ((0, 32),), -0.2, 0.2)), 4096.0, 32768.0)
    gain_second = jnp.clip(jnp.exp(math.log(40960.0) - 2.0794415 * jax.random.uniform(arg_keys[17], (D, 4), jnp.float32) ** block_scale(arg_keys[17], (D, 4), ((0, 32),), -0.2, 0.2)), 5120.0, 40960.0)
    return dict(patches=patches, segments=segments, cotangent=cotangent, qkv_weight=qkv_weight, out_weight=out_weight, in_weight=in_weight, back_weight=back_weight, norm_gains=norm_gains, qkv_first=qkv_first, out_first=out_first, in_first=in_first, back_first=back_first, gain_first=gain_first, qkv_second=qkv_second, out_second=out_second, in_second=in_second, back_second=back_second, gain_second=gain_second)


@jax.custom_vjp
def low(v):
    return lax.optimization_barrier(v.astype(jnp.bfloat16)).astype(jnp.float32)

@jax.custom_vjp
def low_back(v):
    return v

def low_keep(v):
    return (low(v), None)

def low_pass(kept, grad):
    return (grad,)

def back_keep(v):
    return (v, None)

def back_low(kept, grad):
    return (low(grad),)
low.defvjp(low_keep, low_pass)
low_back.defvjp(back_keep, back_low)
pad_mark = 7
beta_one = 0.5
beta_two = 0.5
epsilon = 1e-08
rate_list = (0.03, 0.1, 0.03, 0.02, 0.1)
shrink_list = (0.1, 0.1, 0.1, 0.1, 0.0)
highest = lax.Precision.HIGHEST

def normalize(value, gain):
    centre = lax.optimization_barrier(jnp.mean(value, axis=-1, keepdims=True))
    centred = value - centre
    spread = lax.optimization_barrier(jnp.mean(centred * centred, axis=-1, keepdims=True))
    return centred * lax.rsqrt(spread + 1e-06) * gain

def attend(block):
    queries, keys_all, values_all, seg_row = block
    same_image = seg_row[:, None] == seg_row[None, :]
    scores = jnp.einsum('qhd,khd->hqk', queries, keys_all, precision=highest) * HD ** (-0.5)
    scores = low_back(scores)
    scores = jnp.where(same_image[None], scores, -1e+30)
    attn_probs = low(jax.nn.softmax(scores, axis=-1))
    return jnp.einsum('hqk,khd->qhd', attn_probs, values_all, precision=highest)

def forward(inputs, qkv_weight, out_weight, in_weight, back_weight, norm_gains, segments, live_rows):
    gain_set = low(norm_gains)
    normed_one = low(normalize(inputs, gain_set[:, 0]))
    projected = low_back(jnp.einsum('gtd,de->gte', normed_one, low(qkv_weight), precision=highest))
    shape = (GROUPS, ROW, H, HD)
    queries = low(normalize(projected[..., :D].reshape(shape), gain_set[:, 2].reshape(H, HD)))
    keys_all = low(normalize(projected[..., D:2 * D].reshape(shape), gain_set[:, 3].reshape(H, HD)))
    values_all = low(projected[..., 2 * D:].reshape(shape))
    mixed = lax.map(jax.checkpoint(attend), (queries, keys_all, values_all, segments))
    mixed = low(low_back(mixed.reshape(GROUPS, ROW, D) * live_rows[..., None]))
    after = inputs + low_back(jnp.einsum('gtd,de->gte', mixed, low(out_weight), precision=highest))
    normed_two = low(normalize(after, gain_set[:, 1]))
    hidden = low_back(jnp.einsum('gtd,df->gtf', normed_two, low(in_weight), precision=highest))
    activated = low(jax.nn.gelu(hidden))
    return after + low_back(jnp.einsum('gtf,fd->gtd', activated, low(back_weight), precision=highest))

def adam_step(weight, grad, first, second, rate, shrink):
    first_new = beta_one * first + (1.0 - beta_one) * grad
    second_new = beta_two * second + (1.0 - beta_two) * grad * grad
    first_fix = first_new / (1.0 - beta_one ** STEP)
    second_fix = second_new / (1.0 - beta_two ** STEP)
    weight_new = weight - rate * (first_fix / (jnp.sqrt(second_fix) + epsilon) + shrink * weight)
    return (first_new, second_new, weight_new)

def reference(patches, segments, cotangent, qkv_weight, out_weight, in_weight, back_weight, norm_gains, qkv_first, out_first, in_first, back_first, gain_first, qkv_second, out_second, in_second, back_second, gain_second):
    live_rows = (segments != pad_mark).astype(jnp.float32)
    inputs = patches.astype(jnp.float32)

    def run(input_value, qkv_value, out_value, in_value, back_value, gain_value):
        return forward(input_value, qkv_value, out_value, in_value, back_value, gain_value, segments, live_rows)
    result, pull = jax.vjp(run, inputs, qkv_weight, out_weight, in_weight, back_weight, norm_gains)
    grads = pull(cotangent.astype(jnp.float32))
    qkv_moment, qkv_square, qkv_new = adam_step(qkv_weight, grads[1], qkv_first, qkv_second, rate_list[0], shrink_list[0])
    out_moment, out_square, out_new = adam_step(out_weight, grads[2], out_first, out_second, rate_list[1], shrink_list[1])
    in_moment, in_square, in_new = adam_step(in_weight, grads[3], in_first, in_second, rate_list[2], shrink_list[2])
    back_moment, back_square, back_new = adam_step(back_weight, grads[4], back_first, back_second, rate_list[3], shrink_list[3])
    gain_moment, gain_square, gain_new = adam_step(norm_gains, grads[5], gain_first, gain_second, rate_list[4], shrink_list[4])
    return (result.astype(jnp.bfloat16), grads[0].astype(jnp.bfloat16), qkv_moment, qkv_square, qkv_new, out_moment, out_square, out_new, in_moment, in_square, in_new, back_moment, back_square, back_new, gain_moment, gain_square, gain_new)
```

```python
import functools

import jax
import jax.numpy as jnp
from jax import lax
from jax.experimental import pallas as pl
from jax.experimental.pallas import tpu as pltpu
from jax.sharding import PartitionSpec as P

H = 12
HD = 64
STEP = 5
SPAN = 16
NZ = 4

pad_mark = 7
beta_one = 0.5
beta_two = 0.5
epsilon = 1e-08
rate_list = (0.03, 0.1, 0.03, 0.02, 0.1)
shrink_list = (0.1, 0.1, 0.1, 0.1, 0.0)

MESH = pl.DeviceIdType.MESH
f32 = jnp.float32
bf16 = jnp.bfloat16
LONG = 1024
KB = 256
VMEM_BYTES = 66 * 2**20 - 2**19


def dot(a, b):
    return lax.dot_general(a, b, (((1,), (0,)), ((), ())), preferred_element_type=f32)


def dot_nt(a, b):
    return lax.dot_general(a, b, (((1,), (1,)), ((), ())), preferred_element_type=f32)


def dot_tn(a, b):
    return lax.dot_general(a, b, (((0,), (0,)), ((), ())), preferred_element_type=f32)


def split_dot(value, matrix):
    high = value.astype(bf16)
    rest = (value - high.astype(f32)).astype(bf16)
    return dot(high, matrix) + dot(rest, matrix)


def lanes(shape):
    return lax.broadcasted_iota(jnp.int32, shape, len(shape) - 1)


def head_matrix(width, scale, swap):
    row = lax.broadcasted_iota(jnp.int32, (width, width), 0) // HD
    col = lax.broadcasted_iota(jnp.int32, (width, width), 1) // HD
    if swap:
        col = col + 1 - 2 * (col % 2)
    return jnp.where(row == col, scale, 0.0).astype(bf16)


def loop(count, body, steps=()):
    def one(i, carry):
        for at, step in steps:
            pl.when(i == at)(step)
        body(i)
        return carry

    lax.fori_loop(0, count, one, 0)


class Wires:
    def __init__(self, send_sems, recv_sems):
        self.send_sems, self.recv_sems = send_sems, recv_sems
        self.names = {}
        self.size = 0
        self.pending = {}

    def at(self, name, count=1):
        if name not in self.names:
            self.names[name] = self.size
            self.size += count
        return self.names[name]

    def make(self, send_at, recv_at, src, dst, dev):
        return pltpu.make_async_remote_copy(
            src_ref=src,
            dst_ref=dst,
            send_sem=self.send_sems.at[send_at],
            recv_sem=self.recv_sems.at[recv_at],
            device_id=dev,
            device_id_type=MESH,
        )

    def send(self, name, src, dst, dev):
        i = self.at(name)
        self.send_at(i, i, src, dst, dev)

    def send_at(self, send_at, recv_at, src, dst, dev):
        self.make(send_at, recv_at, src, dst, dev).start()
        self.pending[send_at] = lambda: self.make(send_at, recv_at, src, dst, dev).wait_send()

    def recv(self, name, dst, dev):
        self.recv_at(self.at(name), dst, dev)

    def recv_at(self, at, dst, dev):
        self.make(at, at, dst, dst, dev).wait_recv()

    def send_or_keep(self, remote, send_at, recv_at, src, dst, kept, dev):
        def far():
            self.make(send_at, recv_at, src, dst, dev).start()

        def near():
            pltpu.make_async_copy(src, kept, self.recv_sems.at[recv_at]).start()

        pl.when(remote)(far)
        pl.when(jnp.logical_not(remote))(near)

        def finish():
            pl.when(remote)(lambda: self.make(send_at, recv_at, src, dst, dev).wait_send())

        self.pending[send_at] = finish

    def sent(self, name):
        self.pending.pop(self.at(name))()

    def drain(self):
        for finish in self.pending.values():
            finish()
        self.pending = {}


def layer_kernel(
    count,
    patch_in, cot_in, feat_in, wq_in, wo_in, wi_in, wb_in, gain_in,
    block_out, patch_out, gq_out, go_out, gi_out, gb_out, gg_out,
    xs, ys, feat_rx, feat, sq, so, si, rq, ro, ri, wq, wo, wi, wb, gains, gains_rx,
    a_all, cen, qn, kn, vn, o_all, inv, x1, b_all, act, gp, tx, rx_a, rx_b,
    do_all, dqp, dkp, dvp, ggrad, ggrad_rx,
    go, gi, gb, r1q, r1o, r1i, r1b, r2q, r2o, r2i, r2b, r3q, r3o, r3i, r3b,
    fq, fo, fi, uq, uo, ui,
    send_sems, recv_sems,
):
    rows, width = xs.shape
    full = a_all.shape[0]
    half = width // 2
    ff = wi.shape[1]
    pairs = half // 128
    dp, y = lax.axis_index("dp"), lax.axis_index("blk")
    base = dp // SPAN * SPAN
    z, x, c = dp % SPAN // 4, dp % 4 // 2, dp % 2
    ny, nx, nc = 1 - y, 1 - x, 1 - c
    swapped = c != y

    def dev(z_, x_, c_, y_):
        return (base + (z_ * 2 + x_) * 2 + c_, y_)

    sib = dev(z, x, nc, y)
    ynb = dev(z, x, c, ny)
    xnb = dev(z, nx, c, y)
    diag = dev(z, x, nc, ny)
    zs = [dev((z + d) % NZ, x, c, y) for d in range(NZ)]
    wires = Wires(send_sems, recv_sems)
    send, recv = wires.send, wires.recv

    barrier = pltpu.get_barrier_semaphore()
    partners = [sib, ynb, xnb, diag] + zs[1:]
    for partner in partners:
        pl.semaphore_signal(barrier, inc=1, device_id=partner, device_id_type=MESH)
    pl.semaphore_wait(barrier, len(partners))

    own_rows = pl.ds(pl.multiple_of(c * rows, 128), rows)
    sib_rows = pl.ds(pl.multiple_of(nc * rows, 128), rows)
    head_rows = pl.ds(pl.multiple_of(c * half, 128), half)

    def block(z_, x_, y_):
        return (z_ * 2 + x_) * 2 + y_

    class Matrix:
        def __init__(self, name, weight, grad, first, second, third, order):
            self.name = name
            self.rx1 = [[first.at[d, r] for r in range(2)] for d in range(NZ)]
            self.rx2 = [second.at[d] for d in range(NZ)]
            self.rx3 = [third.at[d] for d in range(NZ - 1)]
            o, no = order, 1 - order
            self.depth = weight.shape[0] // SPAN
            xf, yf = x + o - 2 * x * o, y + no - 2 * y * no
            xs_, ys_ = x + no - 2 * x * no, y + o - 2 * y * o
            self.near, self.next = dev(z, xf, c, yf), dev(z, xs_, c, ys_)
            back = [(z + NZ - d) % NZ for d in range(NZ)]
            ahead = [(z + d) % NZ for d in range(NZ)]
            self.at_z = [self.at(weight, block(zd, x, y)) for zd in back]
            self.at_near = [self.at(weight, block(zd, xf, yf)) for zd in back]
            self.at_next = [self.at(weight, block(zd, xs_, ys_)) for zd in back]
            self.at_far = [self.at(weight, block(zd, nx, ny)) for zd in back]
            self.to_next = [[self.at(grad, block(zd, xs_, ys_)), self.at(grad, block(zd, nx, ny))] for zd in ahead]
            self.to_near = [self.at(grad, block(zd, xf, yf)) for zd in ahead]
            self.to_z = [self.at(grad, block(zd, x, y)) for zd in ahead]

        def at(self, ref, b):
            return ref.at[pl.ds(pl.multiple_of(b * self.depth, 16), self.depth)]

        def gather_own(self):
            piece = self.at_z[0]
            for d in range(1, NZ):
                send(f"{self.name}z{d}", piece, piece, zs[d])
            send(f"{self.name}f0", piece, piece, self.near)
            send(f"{self.name}s0", piece, piece, self.next)

        def gather_z(self, d):
            piece = self.at_z[d]
            recv(f"{self.name}z{d}", piece, zs[1])
            send(f"{self.name}f{d}", piece, piece, self.near)
            send(f"{self.name}s{d}", piece, piece, self.next)

        def gather_near(self, d):
            piece = self.at_near[d]
            recv(f"{self.name}f{d}", piece, self.near)
            send(f"{self.name}g{d}", piece, piece, self.next)

        def gather_end(self):
            for d in range(NZ):
                recv(f"{self.name}s{d}", self.at_next[d], self.next)
                recv(f"{self.name}g{d}", self.at_far[d], self.next)

        def gather_steps(self):
            return [functools.partial(self.gather_z, d) for d in (1, 2, 3)] + [
                functools.partial(self.gather_near, d) for d in (0, 1, 2, 3)
            ]

        def reduce_start(self):
            for d in (1, 2, 3, 0):
                for r in (1, 0):
                    send(f"{self.name}a{d}{r}", self.to_next[d][r], self.rx1[d][r], self.next)

        def add(self, piece, landed):
            piece[...] = (piece[...].astype(f32) + landed[...].astype(f32)).astype(bf16)

        def reduce_next(self, d):
            recv(f"{self.name}a{d}1", self.rx1[d][1], self.next)
            self.add(self.to_near[d], self.rx1[d][1])
            send(f"{self.name}b{d}", self.to_near[d], self.rx2[d], self.near)
            recv(f"{self.name}a{d}0", self.rx1[d][0], self.next)
            self.add(self.to_z[d], self.rx1[d][0])

        def reduce_near(self, d):
            recv(f"{self.name}b{d}", self.rx2[d], self.near)
            self.add(self.to_z[d], self.rx2[d])
            if d:
                send(f"{self.name}c{d}", self.to_z[d], self.rx3[d - 1], zs[d])

        def reduce_end(self):
            total = self.to_z[0][...].astype(f32)
            for d in range(1, NZ):
                recv(f"{self.name}c{d}", self.rx3[d - 1], zs[1])
                total = total + self.rx3[d - 1][...].astype(f32)
            return total

        def reduce_steps(self):
            out = []
            for d in (1, 2, 3, 0):
                out.append(functools.partial(self.reduce_next, d))
            for d in (1, 2, 3, 0):
                out.append(functools.partial(self.reduce_near, d))
            return out

    gq = act.at[pl.ds(0, width), pl.ds(0, wq.shape[1])]
    mq = Matrix("q", wq, gq, r1q, r2q, r3q, 0)
    mo = Matrix("o", wo.at[c], go, r1o, r2o, r3o, c)
    mi = Matrix("i", wi, gi, r1i, r2i, r3i, 0)
    mb = Matrix("b", wb, gb, r1b, r2b, r3b, c)

    def spread(name, staged, landed):
        at = wires.at(f"{name}0", 2)
        wires.send_at(at, at + y, staged.at[nc], landed.at[y], dev(z, x, nc, c))
        wires.send_or_keep(swapped, at + 1, at + y, staged.at[c], landed.at[y], landed.at[y], dev(z, x, c, c))

    def collect(name, landed, matrix):
        at = wires.at(f"{name}0", 2)
        for p in range(2):
            wires.recv_at(at + p, landed.at[p], sib)
        parts = [landed[p].astype(f32)[: matrix.depth // 2] for p in range(2)]
        matrix.at_z[0][...] = jnp.concatenate(parts, 0).astype(bf16)

    def unspread(name, matrix, ready, landed):
        at = wires.at(f"{name}9", 2)
        to, far, near = at + c, dev(z, x, y, ny), dev(z, x, y, y)
        depth = matrix.depth // 2
        other, same, slot = ready.at[ny], ready.at[y], landed.at[c]

        def go_on():
            total = matrix.reduce_end()
            for p in range(2):
                ready[p] = total[p * depth : (p + 1) * depth]
            wires.send_at(at, to, other, slot, far)
            wires.send_or_keep(swapped, at + 1, to, same, slot, slot, near)

        return go_on

    def unspread_end(name, landed, out):
        at = wires.at(f"{name}9", 2)
        for p in range(2):
            wires.recv_at(at + p, landed.at[p], sib)
        out[...] = landed[...]

    def sum_steps(name, own, landed):
        def pass_on(k, partner):
            send(f"{name}{k}", own.at[k], landed.at[k], partner)
            recv(f"{name}{k}", landed.at[k], partner)
            own[k + 1] = own[k] + landed[k]

        def last():
            for d in range(1, NZ):
                send(f"{name}z{d}", own.at[3], landed.at[2 + d], zs[d])
            total = own[3]
            for d in range(1, NZ):
                recv(f"{name}z{d}", landed.at[2 + d], zs[1])
                total = total + landed[2 + d]
            own[4] = total

        return [functools.partial(pass_on, k, who) for k, who in enumerate((sib, ynb, xnb))] + [last]

    def run(steps):
        for step in steps:
            step()

    for name, source, staged, landed in (("q", wq_in, sq, rq), ("o", wo_in, so, ro)):
        part = source.shape[1] // 6 if name == "q" else source.shape[1] // 2
        kinds = 3 if name == "q" else 1
        staged[...] = jnp.zeros_like(staged)
        for h in range(2):
            for kind in range(kinds):
                take = source[:, pl.ds((kind * 2 + h) * part, part)]
                pad = jnp.zeros((staged.shape[1] - take.shape[0], part), f32)
                staged[h, :, pl.ds(kind * part, part)] = jnp.concatenate([take, pad], 0).astype(bf16)
        spread(name, staged, landed)
    at_x = wires.at("xs")
    wires.send_or_keep(swapped, at_x, at_x, patch_in, xs, xs, diag)
    send("feat", feat_in, feat_rx, sib)
    gains[0] = gain_in[...].astype(bf16).astype(f32)
    gain_steps = sum_steps("gain", gains, gains_rx)

    group = ff // 8
    for pair in range(4):
        even = wi_in[:, pl.ds(4 * pair * group, 2 * group)]
        odd = wi_in[:, pl.ds((4 * pair + 2) * group, 2 * group)]
        low_lane = lanes(even.shape) < group
        first = jnp.where(low_lane, even, pltpu.roll(odd, group, 1))
        second = jnp.where(low_lane, pltpu.roll(even, group, 1), odd)
        pad = jnp.zeros((si.shape[1] - even.shape[0], 2 * group), f32)
        for h, value in enumerate((first, second)):
            si[h, :, pl.ds(2 * pair * group, 2 * group)] = jnp.concatenate([value, pad], 0).astype(bf16)
    spread("i", si, ri)
    mb.at_z[0][...] = wb_in[...].astype(bf16)

    collect("q", rq, mq)
    mq.gather_own()
    gain_steps[0]()
    recv("feat", feat_rx, sib)
    feat[...] = jnp.where(swapped, feat_rx[...], feat_in[...])
    gain_steps[1]()
    mq.gather_z(1)
    gain_steps[2]()
    mq.gather_z(2)
    mq.gather_z(3)
    gain_steps[3]()
    gain_first, gain_second = gains[4, 0:1, :], gains[4, 1:2, :]
    recv("xs", xs, diag)

    def norm_one(i):
        v = xs[pl.ds(pl.multiple_of(i * 128, 128), 128)].astype(f32)
        centred = v - jnp.mean(v, axis=-1, keepdims=True)
        spread_ = jnp.mean(centred * centred, axis=-1, keepdims=True)
        normed = centred * lax.rsqrt(spread_ + 1e-6) * gain_first
        a_all[pl.ds(pl.multiple_of(c * rows + i * 128, 128), 128)] = normed.astype(bf16)

    loop(rows // 128, norm_one)
    send("a", a_all.at[own_rows], a_all.at[own_rows], sib)
    for d in range(4):
        mq.gather_near(d)
    collect("o", ro, mo)
    mo.gather_own()
    collect("i", ri, mi)
    mi.gather_own()
    at_y = wires.at("ys")
    wires.send_or_keep(swapped, at_y, at_y, cot_in, ys.at[sib_rows], ys.at[own_rows], diag)
    recv("a", a_all.at[sib_rows], sib)
    mq.gather_end()

    mean_heads = head_matrix(half, 1.0 / HD, False)
    gain_query = gains[4, 2:3, :half] * (1 - c).astype(f32) + gains[4, 2:3, half:] * c.astype(f32)
    gain_key = gains[4, 3:4, :half] * (1 - c).astype(f32) + gains[4, 3:4, half:] * c.astype(f32)

    def project(i):
        at = pl.ds(pl.multiple_of(i * 256, 256), 256)
        projected = dot(a_all[at], wq[...])
        for part, gain, to in ((0, gain_query, qn), (1, gain_key, kn)):
            value = projected[:, part * half : (part + 1) * half]
            centred = value - split_dot(value, mean_heads)
            spread_ = dot((centred * centred).astype(bf16), mean_heads)
            cen[at, pl.ds(part * half, half)] = centred.astype(bf16)
            normed = (centred * lax.rsqrt(spread_ + 1e-6) * gain).astype(bf16)
            to[at] = normed * (HD**-0.5) if part == 0 else normed
        vn[at] = projected[:, 2 * half :].astype(bf16)

    loop(full // 256, project, list(enumerate(mo.gather_steps()[:5])))
    run(mo.gather_steps()[5:])

    low_head = lambda shape: lanes(shape) < HD

    def head_pair(ref, at, p):
        return ref[at, pl.ds(pl.multiple_of(p * 128, 128), 128)]

    def masks(at):
        one_hot = feat[at]
        return one_hot, (one_hot.astype(f32) * 128.0 - 128.0).astype(bf16)

    def attend(p, q_at, k_at):
        q, k, v = head_pair(qn, q_at, p), head_pair(kn, k_at, p), head_pair(vn, k_at, p)
        fq_, _ = masks(q_at)
        _, fk = masks(k_at)
        out = []
        for parity in range(2):
            mine = lambda a, b: jnp.where(low_head(a.shape) == (parity == 0), a, b)
            scores = dot_nt(mine(q, fq_), mine(k, fk))
            weights = jnp.exp(scores).astype(bf16)
            out.append(dot(weights, mine(v, jnp.ones_like(v))))
        return out

    def finish_attend(p, at, r0, r1):
        low = low_head(r0.shape)
        inverse = 1.0 / pltpu.roll(jnp.where(low, r1, r0), HD, 1)
        live = 1.0 - feat[at][:, pad_mark : pad_mark + 1].astype(f32)
        lane_at = pl.ds(pl.multiple_of(p * 128, 128), 128)
        inv[at, lane_at] = inverse
        o_all[c, at, lane_at] = (jnp.where(low, r0, r1) * inverse * live).astype(bf16)

    long_at, short_at = pl.ds(0, LONG), pl.ds(LONG, full - LONG)
    blocks = LONG // KB

    def attend_step(t):
        p, kb = t // blocks, t % blocks
        r0, r1 = attend(p, long_at, pl.ds(pl.multiple_of(kb * KB, KB), KB))

        @pl.when(kb == 0)
        def _():
            dkp[long_at] = r0
            dvp[long_at] = r1

        @pl.when(kb > 0)
        def _():
            dkp[long_at] += r0
            dvp[long_at] += r1

        @pl.when(kb == blocks - 1)
        def _():
            finish_attend(p, long_at, dkp[long_at], dvp[long_at])
            s0, s1 = attend(p, short_at, short_at)
            finish_attend(p, short_at, s0, s1)

    loop(pairs * blocks, attend_step, list(enumerate(mi.gather_steps())))
    send("o", o_all.at[c], o_all.at[c], sib)
    mo.gather_end()
    send("wo", wo.at[c], wo.at[c], sib)
    mb.gather_own()
    recv("ys", ys.at[own_rows], diag)
    send("yy", ys.at[own_rows], ys.at[own_rows], sib)
    recv("wo", wo.at[nc], sib)
    recv("o", o_all.at[nc], sib)

    def norm_parts(value, gain):
        centred = value - jnp.mean(value, axis=-1, keepdims=True)
        spread_ = jnp.mean(centred * centred, axis=-1, keepdims=True)
        scale = lax.rsqrt(spread_ + 1e-6)
        return centred * scale, scale

    step_rows = rows // 2

    def project_out(i):
        here = pl.ds(pl.multiple_of(i * step_rows, 64), step_rows)
        there = pl.ds(pl.multiple_of(c * rows + i * step_rows, 64), step_rows)
        o0, o1 = o_all[0, there], o_all[1, there]
        for j in range(2):
            cols = pl.ds(j * half, half)
            mixed = dot(o0, wo[j, pl.ds(0, half)]) + dot(o1, wo[j, pl.ds(half, half)])
            x1[here, cols] = xs[here, cols].astype(f32) + mixed
        normed, _ = norm_parts(x1[here], None)
        b_all[there] = (normed * gain_second).astype(bf16)

    loop(2, project_out)
    send("b", b_all.at[own_rows], b_all.at[own_rows], sib)
    mi.gather_end()
    recv("yy", ys.at[sib_rows], sib)
    recv("b", b_all.at[sib_rows], sib)

    def hidden(n):
        cols = pl.ds(pl.multiple_of(n * 256, 256), 256)
        zed = dot(b_all[...], wi[:, cols])
        root = 0.7978845608028654
        cube = zed * zed
        tanh = jnp.tanh(root * zed * (1.0 + 0.044715 * cube))
        activated = (0.5 * zed * (1.0 + tanh)).astype(bf16)
        slope = 0.5 * (1.0 + tanh) + 0.5 * zed * (1.0 - tanh * tanh) * (root * (1.0 + 0.134145 * cube))
        act[:, cols] = activated
        gp[:, cols] = slope.astype(bf16)
        gb[cols] = dot_tn(activated, ys[...]).astype(bf16)

    loop(ff // 256, hidden, list(enumerate(mb.gather_steps()[:6])))
    run(mb.gather_steps()[6:])
    mb.reduce_start()
    mb.gather_end()

    def tensor_sum(name, lhs, matrix_cols, landed):
        for n in range(width // 256):
            cols = pl.ds(n * 256, 256)
            tx[:, cols] = matrix_cols(lhs(sib_rows), n)
            send(f"{name}{n}", tx.at[:, cols], landed.at[:, cols], sib)

    def out_cols(rows_, n):
        return dot(rows_, wb[:, pl.ds(n * 256, 256)])

    tensor_sum("po", lambda at: act[at, :], out_cols, rx_a)
    for n in range(width // 256):
        cols = pl.ds(n * 256, 256)
        part = out_cols(act[own_rows, :], n)
        recv(f"po{n}", rx_a.at[:, cols], sib)
        rx_a[:, cols] = x1[:, cols] + part + rx_a[:, cols]
    stage = act.at[pl.ds(0, rows), pl.ds(0, width)]
    stage[...] = rx_a[...].astype(bf16)
    at_b = wires.at("bo")
    wires.send_or_keep(swapped, at_b, at_b, stage, block_out, block_out, diag)

    b_steps = mb.reduce_steps()

    def hidden_back(n):
        cols = pl.ds(pl.multiple_of(n * 256, 256), 256)
        grad = (dot_nt(ys[...], wb[cols, :]) * gp[:, cols].astype(f32)).astype(bf16)
        gp[:, cols] = grad
        gi[:, cols] = dot_tn(b_all[...], grad).astype(bf16)

    loop(ff // 256, hidden_back, list(enumerate(b_steps[:6])))
    mi.reduce_start()
    run(b_steps[6:])

    def in_cols(rows_, n):
        return dot_nt(rows_, wi[pl.ds(n * 256, 256), :])

    for n in range(width // 256):
        wires.sent(f"po{n}")
    tensor_sum("pi", lambda at: gp[at, :], in_cols, rx_b)
    for n in range(width // 256):
        cols = pl.ds(n * 256, 256)
        part = in_cols(gp[own_rows, :], n)
        recv(f"pi{n}", rx_b.at[:, cols], sib)
        rx_b[:, cols] = part + rx_b[:, cols]

    ggrad[0] = jnp.zeros_like(ggrad[0])
    wires.sent("b")
    dxb = b_all

    def norm_back(grad, gain, normed, scale):
        lifted = grad * gain
        return scale * (
            lifted
            - jnp.mean(lifted, axis=-1, keepdims=True)
            - normed * jnp.mean(lifted * normed, axis=-1, keepdims=True)
        )

    def second_back(i):
        here = pl.ds(pl.multiple_of(i * 128, 128), 128)
        there = pl.ds(pl.multiple_of(c * rows + i * 128, 128), 128)
        grad = rx_b[here]
        normed, scale = norm_parts(x1[here], None)
        ggrad[0, 1:2, :] += jnp.sum(grad * normed, axis=0, keepdims=True)
        total = ys[there].astype(f32) + norm_back(grad, gain_second, normed, scale)
        x1[here] = total
        dxb[there] = total.astype(bf16)

    loop(rows // 128, second_back)
    send("dx", dxb.at[own_rows], dxb.at[own_rows], sib)
    i_steps = mi.reduce_steps()
    i_steps[0]()
    recv("dx", dxb.at[sib_rows], sib)

    for j in range(2):
        go[pl.ds(j * half, half)] = dot_tn(o_all[j], dxb[:, head_rows]).astype(bf16)
    mo.reduce_start()

    def project_back(i):
        at = pl.ds(pl.multiple_of(i * 256, 256), 256)
        grad = dot_nt(dxb[at, pl.ds(0, half)], wo[0, head_rows]) + dot_nt(
            dxb[at, pl.ds(half, half)], wo[1, head_rows]
        )
        live = 1.0 - feat[at][:, pad_mark : pad_mark + 1].astype(f32)
        do_all[at] = (grad.astype(bf16).astype(f32) * live * inv[at]).astype(bf16)

    loop(full // 256, project_back, list(enumerate(i_steps[1:6])))

    swap_heads = head_matrix(128, 1.0, True)
    pair_mean = head_matrix(128, 1.0 / HD, False)

    def attend_back(p, q_at, k_at, first):
        q, k, v = head_pair(qn, q_at, p), head_pair(kn, k_at, p), head_pair(vn, k_at, p)
        grad = head_pair(do_all, q_at, p)
        lane_at = pl.ds(pl.multiple_of(p * 128, 128), 128)
        product = grad.astype(f32) * o_all[c, q_at, lane_at].astype(f32)
        delta = split_dot(product, swap_heads)
        d0 = delta.astype(bf16).astype(f32)
        d1 = (delta - d0).astype(bf16).astype(f32)
        d2 = delta - d0 - d1
        spot = lanes(delta.shape) % HD
        rider = jnp.where(spot == 0, -d0, jnp.where(spot == 1, -d1, jnp.where(spot == 2, -d2, 0.0))).astype(bf16)
        fq_, _ = masks(q_at)
        _, fk = masks(k_at)
        dqs, dks, dvs = [], [], []
        for parity in range(2):
            mine = lambda a, b: jnp.where(low_head(a.shape) == (parity == 0), a, b)
            weights = jnp.exp(dot_nt(mine(k, fk), mine(q, fq_)))
            slopes = dot_nt(mine(v, jnp.ones_like(v)), mine(grad, rider))
            dscores = (weights * slopes).astype(bf16)
            dvs.append(dot(weights.astype(bf16), grad))
            dks.append(dot(dscores, q))
            dqs.append(dot_tn(dscores, k))
        merge = lambda pair: jnp.where(low_head(pair[0].shape), pair[0], pair[1])
        dqp[q_at] = merge(dqs)
        if first is None:
            dkp[k_at] = merge(dks)
            dvp[k_at] = merge(dvs)
        else:

            @pl.when(first)
            def _():
                dkp[k_at] = merge(dks)
                dvp[k_at] = merge(dvs)

            @pl.when(jnp.logical_not(first))
            def _():
                dkp[k_at] += merge(dks)
                dvp[k_at] += merge(dvs)

    dproj = gp.at[:, pl.ds(0, 3 * half)]

    def head_back(p):
        lane_at = pl.ds(pl.multiple_of(p * 128, 128), 128)

        def some(i):
            at = pl.ds(pl.multiple_of(i * 256, 256), 256)
            for part, source, gain_row, scale_by in ((0, dqp, 2, HD**-0.5), (1, dkp, 3, 1.0)):
                lane_all = pl.ds(pl.multiple_of(c * half + p * 128, 128), 128)
                gain = gains[4, pl.ds(gain_row, 1), lane_all]
                centred = cen[at, pl.ds(pl.multiple_of(part * half + p * 128, 128), 128)].astype(f32)
                scale = lax.rsqrt(dot((centred * centred).astype(bf16), pair_mean) + 1e-6)
                normed = centred * scale
                grad = source[at] * scale_by if part == 0 else source[at]
                ggrad[0, pl.ds(gain_row, 1), lane_all] += jnp.sum(grad * normed, axis=0, keepdims=True)
                lifted = grad * gain
                back = scale * (
                    lifted - split_dot(lifted, pair_mean) - normed * split_dot(lifted * normed, pair_mean)
                )
                dproj[at, pl.ds(pl.multiple_of(part * half + p * 128, 128), 128)] = back.astype(bf16)
            dproj[at, pl.ds(pl.multiple_of(2 * half + p * 128, 128), 128)] = dvp[at].astype(bf16)

        loop(full // 256, some)

    def back_step(t):
        p, qb = t // blocks, t % blocks
        attend_back(p, pl.ds(pl.multiple_of(qb * KB, KB), KB), long_at, qb == 0)

        @pl.when(qb == blocks - 1)
        def _():
            attend_back(p, short_at, short_at, None)
            head_back(p)

    o_steps = mo.reduce_steps()
    later = i_steps[6:] + [unspread("i", mi, fi, ui)] + o_steps

    loop(pairs * blocks, back_step, list(enumerate(later[:12])))
    run(later[12:])
    unspread("o", mo, fo, uo)()
    gb_out[...] = mb.reduce_end()

    wires.sent("bo")
    recv("bo", block_out, diag)
    for part in range(3):
        cols = pl.ds(part * half, half)
        gq[:, cols] = dot_tn(a_all[...], dproj[:, cols]).astype(bf16)
    mq.reduce_start()

    def first_cols(rows_, n):
        return dot_nt(rows_, wq[pl.ds(n * 256, 256), :])

    for n in range(width // 256):
        wires.sent(f"pi{n}")
    tensor_sum("pq", lambda at: dproj[at, :], first_cols, rx_a)
    q_steps = mq.reduce_steps()
    for n in range(width // 256):
        cols = pl.ds(n * 256, 256)
        part = first_cols(dproj[own_rows, :], n)
        recv(f"pq{n}", rx_a.at[:, cols], sib)
        rx_a[:, cols] = part + rx_a[:, cols]
    q_steps[0]()

    def first_back(i):
        here = pl.ds(pl.multiple_of(i * 128, 128), 128)
        grad = rx_a[here]
        normed, scale = norm_parts(xs[here].astype(f32), None)
        ggrad[0, 0:1, :] += jnp.sum(grad * normed, axis=0, keepdims=True)
        total = x1[here] + norm_back(grad, gain_first, normed, scale)
        xs[here] = total.astype(bf16)

    loop(rows // 128, first_back)
    at_p = wires.at("pg")
    wires.send_or_keep(swapped, at_p, at_p, xs, patch_out, patch_out, diag)
    q_steps[1]()
    grad_steps = sum_steps("gg", ggrad, ggrad_rx)
    run(q_steps[2:4])
    grad_steps[0]()
    run(q_steps[4:6])
    grad_steps[1]()
    run(q_steps[6:])
    grad_steps[2]()
    unspread("q", mq, fq, uq)()
    grad_steps[3]()
    gg_out[...] = ggrad[4]
    unspread_end("i", ui, gi_out)
    unspread_end("o", uo, go_out)
    unspread_end("q", uq, gq_out)
    recv("pg", patch_out, diag)
    wires.drain()
    count.append(wires.size)


def run_layer(patches, cotangent, feat, weights, gain_rows):
    rows, width = patches.shape
    full = feat.shape[0]
    half = width // 2
    wq_in, wo_in, wi_in, wb_in = weights
    shard = wq_in.shape[0]
    padded = -(-shard // 16) * 16
    nq, no, ni = wq_in.shape[1] // 2, wo_in.shape[1] // 2, wi_in.shape[1] // 2
    nb = wb_in.shape[1]
    depth, deep = 2 * shard, wb_in.shape[0]
    vm = lambda shape, kind=bf16: pltpu.VMEM(shape, kind)
    wide = (nq, no, ni)
    scratch = (
        [vm((rows, width)), vm((full, width)), vm((full, 128)), vm((full, 128))]
        + [vm((2, padded, n)) for n in wide] * 2
        + [vm((width, nq)), vm((2, width, no)), vm((width, ni)), vm((SPAN * deep, nb))]
        + [vm((5, 8, width), f32), vm((6, 8, width), f32)]
        + [vm((full, width)), vm((full, width)), vm((full, half)), vm((full, half)), vm((full, half))]
        + [vm((2, full, half)), vm((full, half), f32), vm((rows, width), f32), vm((full, width))]
        + [vm((full, ni)), vm((full, ni))]
        + [vm((rows, width), f32)] * 3
        + [vm((full, half))]
        + [vm((full, 128), f32)] * 3
        + [vm((5, 8, width), f32), vm((6, 8, width), f32)]
        + [vm((width, no)), vm((width, ni)), vm((SPAN * deep, nb))]
        + [vm((NZ, 2, depth, n)) for n in wide] + [vm((NZ, 2, deep, nb))]
        + [vm((NZ, depth, n)) for n in wide] + [vm((NZ, deep, nb))]
        + [vm((NZ - 1, depth, n)) for n in wide] + [vm((NZ - 1, deep, nb))]
        + [vm((2, shard, n), f32) for n in wide] * 2
        + [pltpu.SemaphoreType.DMA((200,)), pltpu.SemaphoreType.DMA((200,))]
    )
    here = pl.BlockSpec(memory_space=pltpu.VMEM)
    away = pl.BlockSpec(memory_space=pl.ANY)
    out = lambda shape, kind=f32: jax.ShapeDtypeStruct(shape, kind)
    return pl.pallas_call(
        functools.partial(layer_kernel, []),
        out_shape=(
            out((rows, width), bf16),
            out((rows, width), bf16),
            out((2, shard, nq)),
            out((2, shard, no)),
            out((2, shard, ni)),
            out((deep, nb)),
            out((8, width)),
        ),
        in_specs=[away, away] + [here] * 6,
        out_specs=(away, away) + (here,) * 5,
        scratch_shapes=scratch,
        compiler_params=pltpu.CompilerParams(
            collective_id=0, has_side_effects=True, vmem_limit_bytes=VMEM_BYTES
        ),
        name="layer",
    )(patches, cotangent, feat, wq_in, wo_in, wi_in, wb_in, gain_rows)


def adam_step(weight, grad, first, second, rate, shrink):
    first_new = beta_one * first + (1.0 - beta_one) * grad
    second_new = beta_two * second + (1.0 - beta_two) * grad * grad
    first_fix = first_new / (1.0 - beta_one**STEP)
    second_fix = second_new / (1.0 - beta_two**STEP)
    weight_new = weight - rate * (first_fix / (jnp.sqrt(second_fix) + epsilon) + shrink * weight)
    return (first_new, second_new, weight_new)


def shards(spans, patches, segments, cotangent, *state):
    weights, first, second = state[:5], state[5:10], state[10:]
    dp, blk = lax.axis_index("dp"), lax.axis_index("blk")
    index = dp * 2 + blk
    width = patches.shape[2]
    members = 2 * SPAN
    place = index % members
    shard = width // members

    def span_rows(weight):
        if spans == 1:
            return weight
        whole = lax.all_gather(weight, ("dp", "blk"), axis=0, tiled=True)
        depth = whole.shape[0] // members
        return lax.dynamic_slice_in_dim(whole, place * depth, depth, 0)

    def span_sum(grad, rows):
        if spans == 1:
            return grad
        whole = jnp.zeros((grad.shape[0] * members, grad.shape[1]), f32)
        whole = lax.dynamic_update_slice_in_dim(whole, grad, place * grad.shape[0], 0)
        whole = lax.psum(whole, ("dp", "blk"))
        return lax.dynamic_slice_in_dim(whole, index * rows, rows, 0)

    seg = segments[0]
    one_hot = (lax.broadcasted_iota(jnp.int32, (seg.shape[0], 128), 1) % HD) == seg[:, None]
    gains = span_rows(weights[4])
    lane = lax.broadcasted_iota(jnp.int32, (4, width), 1)
    gain_rows = jnp.where(lane // shard == place, jnp.tile(gains.T, (1, members)), 0.0)
    gain_rows = jnp.concatenate([gain_rows, jnp.zeros((4, width), f32)], 0)
    block_out, patch_grad, gq, go, gi, gb, gg = run_layer(
        patches[0],
        cotangent[0],
        one_hot.astype(bf16),
        [span_rows(w) for w in weights[:4]],
        gain_rows,
    )
    nq, no, ni = gq.shape[2], go.shape[2], gi.shape[2]
    part = nq // 3
    group = ni // 8
    grads = (
        gq.reshape(2, shard, 3, part).transpose(1, 2, 0, 3).reshape(shard, 2 * nq),
        go.transpose(1, 0, 2).reshape(shard, 2 * no),
        gi.reshape(2, shard, 8, group).transpose(1, 2, 0, 3).reshape(shard, 2 * ni),
        gb,
        lax.dynamic_slice_in_dim(gg[:4], place * shard, shard, 1).T,
    )
    news = []
    for weight, grad, one, two, rate, shrink in zip(weights, grads, first, second, rate_list, shrink_list):
        news += adam_step(weight, span_sum(grad, weight.shape[0]), one, two, rate, shrink)
    return (block_out[None], patch_grad[None], *news)


def solution(mesh):
    rows, tokens = P(("dp", "blk"), None), P("dp", "blk", None)
    return jax.shard_map(
        functools.partial(shards, mesh.shape["dp"] // SPAN),
        mesh=mesh,
        in_specs=(tokens, P("dp", None), tokens) + (rows,) * 15,
        out_specs=(tokens, tokens) + (rows,) * 15,
        check_vma=False,
    )
```

```python
import functools

import jax
import jax.numpy as jnp
from jax import lax
from jax.experimental import pallas as pl
from jax.experimental.pallas import tpu as pltpu
from jax.sharding import PartitionSpec as P

H = 12
HD = 64
STEP = 5
SPAN = 16
NZ = 4

pad_mark = 7
beta_one = 0.5
beta_two = 0.5
epsilon = 1e-08
rate_list = (0.03, 0.1, 0.03, 0.02, 0.1)
shrink_list = (0.1, 0.1, 0.1, 0.1, 0.0)

MESH = pl.DeviceIdType.MESH
f32 = jnp.float32
bf16 = jnp.bfloat16
LONG = 1024
KB = 512
PLAN = {
    "LN1": ("prep", "so", "sq", "hy0", "feat", "co", "featr", "si", "hy1", "hz0", "cq", "q1z", "xs", "hz1", "ci", "oz", "q2n", "q0z", "bn", "in", "q1n", "q2z", "hx0", "q2.g1", "q0.g1", "hx1", "q1.g0", "q1.g2", "iz", "q2.g0", "o.g2", "q1.g3", "q2.g2", "q0n", "q0.g0", "q1.g4", "q2.g3", "on", "o.g0", "q1.g6", "q0.g2", "hs0", "o.g1", "q0.g5", "bz", "hs1", "q0.g3", "q0.g4",),
    "F0": ("q1.g1", "q0.g6", "q2.g4", "i.g2", "b.g3", "q2.g5", "q2.g6", "q1.g5", "ys", "q0.end", "i.g3", "i.g1", "ar",),
    "F1": ("i.g0",),
    "F2": ("o.g6", "o.g4", "o.g5", "o.g3", "q2.end", "q1.end", "b.g0",),
    "OUT": ("i.g4", "o.end", "share", "b.g2", "i.g5", "i.g6", "ysr",),
    "H0": ("b.g1", "b.g4", "b.g6", "i.end",),
    "H2": ("b.g5",),
    "DZ": ("b.rs", "b.end",),
    "PO": ("b.a3", "b.a1", "i.rs",),
    "PB": ("b.a0", "finish", "b.a2",),
    "B0": ("o.rs",),
    "B2": ("i.a1", "q0.rs", "o.a3", "o.a0",),
    "B3": ("o.a2", "o.a1", "b.r0",),
    "B4": ("q0.a0", "q1.rs", "q0.a2", "i.a0", "i.a3", "q0.a1", "i.a2", "i.r1",),
    "PQ": ("q1.a0", "q0.a3", "q0.r0", "o.r0", "i.r2", "q2.rs",),
    "PQEND": ("q0.e", "i.r0", "o.e",),
    "FIRST": ("q2.a2",),
    "END": ("q2.a0", "q2.a1", "ths0", "q2.a3", "ths1", "q1.a3", "q1.a1", "q2.r0", "q1.a2", "i.r3", "i.e", "thx0", "thx1", "o.p", "q0.p", "thz0", "q1.r0", "q2.e", "thz1", "thy0", "b.e", "q1.e", "q2.p", "i.p", "thy1", "q1.p",),
}
VMEM_BYTES = 66 * 2**20 - 2**19
SEMAPHORES = 170


def dot(a, b):
    return lax.dot_general(a, b, (((1,), (0,)), ((), ())), preferred_element_type=f32)


def dot_nt(a, b):
    return lax.dot_general(a, b, (((1,), (1,)), ((), ())), preferred_element_type=f32)


def dot_tn(a, b):
    return lax.dot_general(a, b, (((0,), (0,)), ((), ())), preferred_element_type=f32)


def split_dot(value, matrix):
    high = value.astype(bf16)
    rest = (value - high.astype(f32)).astype(bf16)
    return dot(high, matrix) + dot(rest, matrix)


def lanes(shape):
    return lax.broadcasted_iota(jnp.int32, shape, len(shape) - 1)


def head_matrix(width, scale, swap):
    row = lax.broadcasted_iota(jnp.int32, (width, width), 0) // HD
    col = lax.broadcasted_iota(jnp.int32, (width, width), 1) // HD
    if swap:
        col = col + 1 - 2 * (col % 2)
    return jnp.where(row == col, scale, 0.0).astype(bf16)


def loop(count, body, before=()):
    def one(i, carry):
        for at, steps in enumerate(before):
            if steps:
                pl.when(i == at)(functools.partial(run, steps))
        body(i)
        return carry

    lax.fori_loop(0, count, one, 0)


def run(steps):
    for step in steps:
        step()


class Wires:
    def __init__(self, send_sems, recv_sems):
        self.send_sems, self.recv_sems = send_sems, recv_sems
        self.names = {}
        self.sizes = [0, 0]
        self.pending = {}

    def at(self, name, side, count=1):
        if (name, side) not in self.names:
            self.names[name, side] = self.sizes[side]
            self.sizes[side] += count
        return self.names[name, side]

    def make(self, send_at, recv_at, src, dst, dev):
        return pltpu.make_async_remote_copy(
            src_ref=src,
            dst_ref=dst,
            send_sem=self.send_sems.at[send_at],
            recv_sem=self.recv_sems.at[recv_at],
            device_id=dev,
            device_id_type=MESH,
        )

    def send(self, name, src, dst, dev):
        self.send_at(self.at(name, 0), self.at(name, 1), src, dst, dev)

    def send_at(self, send_at, recv_at, src, dst, dev):
        self.make(send_at, recv_at, src, dst, dev).start()
        self.pending[send_at] = lambda: self.make(send_at, 0, src, src, dev).wait_send()

    def send_group(self, group, whole, name, src, dst, dev):
        send_at = self.at(group, 0)
        self.make(send_at, self.at(name, 1), src, dst, dev).start()
        self.pending[send_at] = lambda: self.make(send_at, 0, whole, whole, dev).wait_send()

    def recv(self, name, dst, dev):
        self.recv_at(self.at(name, 1), dst, dev)

    def recv_at(self, at, dst, dev):
        self.make(0, at, dst, dst, dev).wait_recv()

    def send_or_keep(self, remote, send_at, recv_at, src, dst, kept, dev):
        def far():
            self.make(send_at, recv_at, src, dst, dev).start()

        def near():
            pltpu.make_async_copy(src, kept, self.recv_sems.at[recv_at]).start()

        pl.when(remote)(far)
        pl.when(jnp.logical_not(remote))(near)

        def finish():
            pl.when(remote)(lambda: self.make(send_at, 0, src, dst, dev).wait_send())

        self.pending[send_at] = finish

    def sent(self, name, count=1):
        for i in range(count):
            self.pending.pop(self.at(name, 0) + i)()

    def drain(self):
        for finish in self.pending.values():
            finish()
        self.pending = {}


def layer_kernel(
    patch_in, cot_in, seg_in, wq_in, wo_in, wi_in, wb_in, gain_in,
    block_out, patch_out, gq_out, go_out, gi_out, gb_out, gg_out,
    xs, ys, feat, wq, wo, wi, wb, gains, gains_rx,
    a_all, cen, qn, kn, vn, o_all, inv, x1, b_all, act, gp, tx, rx_a, rx_b,
    do_all, dqp, dkp, dvp, ggrad, ggrad_rx,
    go, gi, gb, r1q, r1o, r1i, r1b, r2q, r2o, r2i, r2b, r3q, r3o, r3i, r3b,
    fq, fo, fi, uq, uo, ui, fb, fg,
    send_sems, recv_sems,
):
    rows, width = xs.shape
    full = a_all.shape[0]
    half = width // 2
    ff = wi.shape[1]
    pairs = half // 128
    dp, y = lax.axis_index("dp"), lax.axis_index("blk")
    base = dp // SPAN * SPAN
    z, x, c = dp % SPAN // 4, dp % 4 // 2, dp % 2
    ny, nx, nc = 1 - y, 1 - x, 1 - c
    swapped = c != y

    def dev(z_, x_, c_, y_):
        return (base + (z_ * 2 + x_) * 2 + c_, y_)

    sib = dev(z, x, nc, y)
    ynb = dev(z, x, c, ny)
    xnb = dev(z, nx, c, y)
    diag = dev(z, x, nc, ny)
    zs = [dev((z + d) % NZ, x, c, y) for d in range(NZ)]
    wires = Wires(send_sems, recv_sems)
    send, recv = wires.send, wires.recv

    barrier = pltpu.get_barrier_semaphore()
    partners = [sib, ynb, xnb, diag] + zs[1:]
    for partner in partners:
        pl.semaphore_signal(barrier, inc=1, device_id=partner, device_id_type=MESH)

    own_rows = pl.ds(pl.multiple_of(c * rows, 128), rows)
    sib_rows = pl.ds(pl.multiple_of(nc * rows, 128), rows)
    head_rows = pl.ds(pl.multiple_of(c * half, 128), half)

    def block(z_, x_, y_):
        return (z_ * 2 + x_) * 2 + y_

    def turns(o):
        no = 1 - o
        return x + o - 2 * x * o, y + no - 2 * y * no, x + no - 2 * x * no, y + o - 2 * y * o

    class Matrix:
        def __init__(self, name, weight, grad, buffers, order, early, back_order, back_early):
            first, second, third = buffers
            self.name = name
            self.early, self.back_early = early, back_early
            self.rx2_three = second.at[pl.ds(0, 3)]
            self.rx1 = [[first.at[d, r] for r in range(2)] for d in range(NZ)]
            self.rx1_both = [first.at[d] for d in range(NZ)]
            self.rx2 = [second.at[d] for d in range(NZ)]
            self.rx3 = [third.at[d] for d in range(NZ - 1)]
            self.rx3_all = third
            self.depth = weight.shape[0] // SPAN
            self.sent_weight = weight.at[pl.ds(0, 15 * self.depth)]
            self.sent_grad = grad.at[pl.ds(0, 15 * self.depth)]
            self.last_weight = weight.at[pl.ds(0, 8 * self.depth)]
            xf, yf, xs_, ys_ = turns(order)
            self.near, self.next = dev(z, xf, c, yf), dev(z, xs_, c, ys_)
            back = [(z + NZ - d) % NZ for d in range(NZ)]
            ahead = [(z + d) % NZ for d in range(NZ)]
            self.at_z = [self.at(weight, block(zd, x, y)) for zd in back]
            self.at_near = [self.at(weight, block(zd, xf, yf)) for zd in back]
            xf, yf, xs_, ys_ = turns(back_order)
            self.back_near, self.back_next = dev(z, xf, c, yf), dev(z, xs_, c, ys_)
            self.to_next = [[self.at(grad, block(zd, xs_, ys_)), self.at(grad, block(zd, nx, ny))] for zd in ahead]
            self.to_near = [self.at(grad, block(zd, xf, yf)) for zd in ahead]
            self.to_z = [self.at(grad, block(zd, x, y)) for zd in ahead]

        def at(self, ref, b):
            return ref.at[pl.ds(pl.multiple_of(b * self.depth, 16), self.depth)]

        def pass_on(self, name, piece, to):
            wires.send_group(f"{self.name}g", self.sent_weight, f"{self.name}{name}", piece, piece, to)

        def gather_own_z(self):
            for d in range(1, NZ):
                self.pass_on(f"z{d}", self.at_z[0], zs[d])

        def gather_own_near(self):
            self.pass_on("f0", self.at_z[0], self.near)
            self.pass_on("s", self.at_z[0], self.next)

        def gather_own(self):
            self.gather_own_z()
            self.gather_own_near()

        def gather_z(self, d):
            recv(f"{self.name}z{d}", self.at_z[d], zs[1])
            if not self.early:
                self.pass_on(f"f{d}", self.at_z[d], self.near)
            self.pass_on("s", self.at_z[d], self.next)

        def gather_near(self, d):
            recv(f"{self.name}f{d}", self.at_near[d], self.near)
            if self.early and d == 0:
                for k in range(1, NZ):
                    self.pass_on(f"f{k}", self.at_near[0], zs[k])
            self.pass_on("s", self.at_near[d], self.next)

        def gather_end(self):
            recv(f"{self.name}s", self.last_weight, self.next)

        def gather_steps(self):
            from_z = [functools.partial(self.gather_z, d) for d in (1, 2, 3)]
            from_near = [functools.partial(self.gather_near, d) for d in (0, 1, 2, 3)]
            return from_near[:1] + from_z + from_near[1:] if self.early else from_z + from_near

        def back(self, name, piece, landed, to):
            wires.send_group(f"{self.name}r", self.sent_grad, f"{self.name}{name}", piece, landed, to)

        def reduce_start(self):
            for d in (1, 2, 3, 0):
                for r in (1, 0):
                    self.back(f"a{d}", self.to_next[d][r], self.rx1[d][r], self.back_next)

        def add(self, piece, landed):
            piece[...] = (piece[...].astype(f32) + landed[...].astype(f32)).astype(bf16)

        def reduce_next(self, d):
            recv(f"{self.name}a{d}", self.rx1_both[d], self.back_next)
            self.add(self.to_near[d], self.rx1[d][1])
            if not self.back_early:
                self.back(f"b{d}", self.to_near[d], self.rx2[d], self.back_near)
            elif d:
                self.back("e", self.to_near[d], self.rx2[d - 1], zs[d])
            self.add(self.to_z[d], self.rx1[d][0])
            if self.back_early and d:
                self.back("c", self.to_z[d], self.rx3[d - 1], zs[d])

        def reduce_near(self, d):
            recv(f"{self.name}b{d}", self.rx2[d], self.back_near)
            self.add(self.to_z[d], self.rx2[d])
            if d:
                self.back("c", self.to_z[d], self.rx3[d - 1], zs[d])

        def reduce_near_early(self):
            recv(f"{self.name}e", self.rx2_three, zs[1])
            total = self.to_near[0][...].astype(f32)
            for landed in self.rx2[:3]:
                total = total + landed[...].astype(f32)
            self.to_near[0][...] = total.astype(bf16)
            self.back("n", self.to_near[0], self.rx2[3], self.back_near)

        def reduce_end(self):
            recv(f"{self.name}c", self.rx3_all, zs[1])
            total = self.to_z[0][...].astype(f32)
            for landed in self.rx3:
                total = total + landed[...].astype(f32)
            if self.back_early:
                recv(f"{self.name}n", self.rx2[3], self.back_near)
                total = total + self.rx2[3][...].astype(f32)
            return total

        def reduce_steps(self):
            first = [functools.partial(self.reduce_next, d) for d in (1, 2, 3, 0)]
            if self.back_early:
                return first, [self.reduce_near_early]
            return first, [functools.partial(self.reduce_near, d) for d in (1, 2, 3, 0)]

    pair_cols = 3 * 128
    gq = [act.at[pl.ds(0, width), pl.ds(p * pair_cols, pair_cols)] for p in range(pairs)]
    mq = [
        Matrix(
            f"q{p}", wq.at[:, pl.ds(p * pair_cols, pair_cols)], gq[p], (r1q.at[p], r2q.at[p], r3q.at[p]), 0, False, c, True
        )
        for p in range(pairs)
    ]
    mo = Matrix("o", wo.at[c], go, (r1o, r2o, r3o), 0, False, 0, True)
    mi = Matrix("i", wi, gi, (r1i, r2i, r3i), c, True, c, False)
    mb = Matrix("b", wb, gb, (r1b, r2b, r3b), nc, False, c, True)

    padded = -(-wq_in.shape[0] // 16) * 16

    def pieces(at, cols):
        return lambda h: gi.at[pl.ds(pl.multiple_of((2 * at + h) * padded, 16), padded), pl.ds(0, cols)]

    sq, rq = pieces(0, wq.shape[1]), pieces(1, wq.shape[1])
    so, ro = pieces(2, half), pieces(3, half)
    si, ri = pieces(4, ff), pieces(5, ff)

    def spread(name, staged, landed):
        to, at = wires.at(f"{name}first", 1, 2) + y, wires.at(f"{name}first", 0, 2)
        other, same, slot = staged(nc), staged(c), landed(y)
        far, near = dev(z, x, nc, c), dev(z, x, c, c)

        def go_on():
            wires.send_at(at, to, other, slot, far)
            wires.send_or_keep(swapped, at + 1, to, same, slot, slot, near)

        return go_on

    def collect(name, landed, *fills):
        at = wires.at(f"{name}first", 1, 2)
        slots = [landed(p) for p in range(2)]

        def go_on():
            for p in range(2):
                wires.recv_at(at + p, slots[p], sib)
            for matrix, cols in fills:
                fill(slots, matrix, cols)

        return go_on

    def fill(slots, matrix, cols):
        parts = [slot[:, cols].astype(f32)[: matrix.depth // 2] for slot in slots]
        matrix.at_z[0][...] = jnp.concatenate(parts, 0).astype(bf16)

    def unspread(name, matrix, ready, landed):
        to, at = wires.at(f"{name}last", 1, 2), wires.at(f"{name}last", 0, 2)
        far, near = dev(z, x, y, ny), dev(z, x, y, y)
        depth = matrix.depth // 2
        slot_at = to + c
        other, same, slot = ready.at[ny], ready.at[y], landed.at[c]

        def go_on():
            total = matrix.reduce_end()
            for p in range(2):
                ready[p] = total[p * depth : (p + 1) * depth]
            wires.send_at(at, slot_at, other, slot, far)
            wires.send_or_keep(swapped, at + 1, slot_at, same, slot, slot, near)

        return go_on

    def unspread_end(name, landed, out):
        at = wires.at(f"{name}last", 1, 2)
        slots = [landed.at[p] for p in range(2)]
        put = pltpu.make_async_copy(landed, out, wires.recv_sems.at[wires.at(f"{name}out", 1)])
        outputs.append(put)

        def go_on():
            for p in range(2):
                wires.recv_at(at + p, slots[p], sib)
            put.start()

        return go_on

    outputs = []

    def sum_hops(name, own, landed, order):
        own, landed = [own.at[k] for k in range(5)], [landed.at[k] for k in range(7)]

        def one(k, partner):
            def start():
                send(f"{name}{k}", own[k], landed[k], partner)

            def end():
                recv(f"{name}{k}", landed[k], partner)
                own[k + 1][...] = own[k][...] + landed[k][...]

            return start, end

        def along_z(k):
            def start():
                for d in range(1, NZ):
                    send(f"{name}z{d}", own[k], landed[3 + d], zs[d])

            def end():
                total = own[k][...]
                for d in range(1, NZ):
                    recv(f"{name}z{d}", landed[3 + d], zs[1])
                    total = total + landed[3 + d][...]
                own[k + 1][...] = total

            return start, end

        return [along_z(k) if who is None else one(k, who) for k, who in enumerate(order)]

    def place_lanes(depth):
        row = lax.broadcasted_iota(jnp.int32, (depth, width), 0)
        spot = ((z * 2 + x) * 2 + c) * 2 + y
        return lanes((depth, width)) == row + spot * depth

    feat_own, feat_rx = do_all.at[:, pl.ds(0, 128)], do_all.at[:, pl.ds(128, 128)]
    gains[0] = jnp.zeros_like(gains[0])
    spread_gain = jnp.where(place_lanes(gain_in.shape[1]), 1.0, 0.0).astype(bf16)
    gains[0, 0:4, :] = dot(gain_in[...].astype(bf16), spread_gain)
    seg_lane = lax.broadcasted_iota(jnp.int32, (128, full), 0) % HD
    feat_own[...] = jnp.where(seg_lane == seg_in[...], 1.0, 0.0).astype(bf16).T
    depth = wq_in.shape[0]
    pad = jnp.zeros((padded - depth, 128), f32)
    for h in range(2):
        for p in range(pairs):
            for part in range(3):
                take = wq_in[:, pl.ds(part * width + h * half + p * 128, 128)]
                sq(h)[:, pl.ds(p * pair_cols + part * 128, 128)] = jnp.concatenate([take, pad], 0).astype(bf16)
    def prepare():
        pad = jnp.zeros((padded - depth, half), f32)
        for h in range(2):
            so(h)[...] = jnp.concatenate([wo_in[:, pl.ds(h * half, half)], pad], 0).astype(bf16)
        group = ff // 8
        pad = jnp.zeros((padded - depth, 2 * group), f32)
        for pair in range(4):
            even = wi_in[:, pl.ds(4 * pair * group, 2 * group)]
            odd = wi_in[:, pl.ds((4 * pair + 2) * group, 2 * group)]
            low_lane = lanes(even.shape) < group
            first = jnp.where(low_lane, even, pltpu.roll(odd, group, 1))
            second = jnp.where(low_lane, pltpu.roll(even, group, 1), odd)
            for h, value in enumerate((first, second)):
                si(h)[:, pl.ds(2 * pair * group, 2 * group)] = jnp.concatenate([value, pad], 0).astype(bf16)
        mb.at_z[0][...] = wb_in[...].astype(bf16)

    do = {}

    def plan(slot):
        return [do[name] for name in PLAN.get(slot, ())]

    def plans(slot, count):
        return [plan(f"{slot}{t}") for t in range(count)]

    for matrix in (*mq, mo, mi, mb):
        name = matrix.name
        do[f"{name}z"], do[f"{name}n"] = matrix.gather_own_z, matrix.gather_own_near
        do[f"{name}.end"], do[f"{name}.rs"] = matrix.gather_end, matrix.reduce_start
        first_steps, rest_steps = matrix.reduce_steps()
        for kind, steps in (("g", matrix.gather_steps()), ("a", first_steps), ("r", rest_steps)):
            for k, step in enumerate(steps):
                do[f"{name}.{kind}{k}"] = step
    for prefix, hops, keys in (
        ("", sum_hops("gain", gains, gains_rx, (ynb, None, xnb, sib)), "yzxs"),
        ("t", sum_hops("gg", ggrad, ggrad_rx, (sib, xnb, None, ynb)), "sxzy"),
    ):
        for key, (start, end) in zip(keys, hops):
            do[f"{prefix}h{key}0"], do[f"{prefix}h{key}1"] = start, end
    all_cols = slice(None)
    do["sq"], do["so"], do["si"] = spread("q", sq, rq), spread("o", so, ro), spread("i", si, ri)
    do["cq"] = collect("q", rq, *[(mq[p], pl.ds(p * pair_cols, pair_cols)) for p in range(pairs)])
    do["co"], do["ci"] = collect("o", ro, (mo, all_cols)), collect("i", ri, (mi, all_cols))
    do["prep"] = prepare
    xs_at, ys_at = (wires.at("xs", 0), wires.at("xs", 1)), (wires.at("ys", 0), wires.at("ys", 1))
    ys_own, ys_sib, wo_mine, wo_other = ys.at[own_rows], ys.at[sib_rows], wo.at[c], wo.at[nc]
    do["xs"] = lambda: wires.send_or_keep(swapped, *xs_at, patch_in, xs, xs, diag)
    do["ys"] = lambda: wires.send_or_keep(swapped, *ys_at, cot_in, ys_sib, ys_own, diag)
    do["share"] = lambda: send("wo", wo_mine, wo_mine, sib)
    do["feat"] = lambda: send("feat", feat_own, feat_rx, sib)

    def pass_cotangent():
        wires.recv_at(ys_at[1], ys_own, diag)
        send("yy", ys_own, ys_own, sib)

    def pick_feat():
        recv("feat", feat_rx, sib)
        feat[...] = jnp.where(swapped, feat_rx[...], feat_own[...])

    a_sib = a_all.at[sib_rows]
    do["ysr"], do["featr"] = pass_cotangent, pick_feat
    do["ar"] = lambda: recv("a", a_sib, sib)
    ends = [("i", mi, fi, ui, gi_out), ("o", mo, fo, uo, go_out)]
    ends += [(f"q{p}", mq[p], fq.at[p], uq.at[p], gq_out.at[p]) for p in range(pairs)]
    for name, matrix, ready, landed, out in ends:
        do[f"{name}.e"] = unspread(name, matrix, ready, landed)
        do[f"{name}.p"] = unspread_end(name, landed, out)
    put_b = pltpu.make_async_copy(fb, gb_out, wires.recv_sems.at[wires.at("bout", 1)])
    outputs.append(put_b)

    def end_b():
        fb[...] = mb.reduce_end()
        put_b.start()

    do["b.e"] = end_b

    pl.semaphore_wait(barrier, len(partners))
    run(plan("LN1"))
    gain_first, gain_second = gains[4, 0:1, :], gains[4, 1:2, :]
    wires.recv_at(xs_at[1], xs, diag)

    def norm_one(i):
        v = xs[pl.ds(pl.multiple_of(i * 128, 128), 128)].astype(f32)
        centred = v - jnp.mean(v, axis=-1, keepdims=True)
        spread_ = jnp.mean(centred * centred, axis=-1, keepdims=True)
        normed = centred * lax.rsqrt(spread_ + 1e-6) * gain_first
        a_all[pl.ds(pl.multiple_of(c * rows + i * 128, 128), 128)] = normed.astype(bf16)

    loop(rows // 128, norm_one)
    send("a", a_all.at[own_rows], a_all.at[own_rows], sib)
    pair_mean = head_matrix(128, 1.0 / HD, False)

    def project(p):
        lane_at = pl.ds(pl.multiple_of(p * 128, 128), 128)
        lane_all = pl.ds(pl.multiple_of(c * half + p * 128, 128), 128)

        projected = dot(a_all[...], wq[:, pl.ds(pl.multiple_of(p * pair_cols, 128), pair_cols)])
        for part, to in ((0, qn), (1, kn)):
            value = projected[:, part * 128 : (part + 1) * 128]
            centred = value - split_dot(value, pair_mean)
            spread_ = dot((centred * centred).astype(bf16), pair_mean)
            cen[:, pl.ds(pl.multiple_of(part * half + p * 128, 128), 128)] = centred.astype(bf16)
            normed = (centred * lax.rsqrt(spread_ + 1e-6) * gains[4, pl.ds(2 + part, 1), lane_all]).astype(bf16)
            to[:, lane_at] = normed * (HD**-0.5) if part == 0 else normed
        vn[:, lane_at] = projected[:, 256:].astype(bf16)

    low_head = lambda shape: lanes(shape) < HD

    def head_pair(ref, at, p):
        return ref[at, pl.ds(pl.multiple_of(p * 128, 128), 128)]

    def masks(at):
        one_hot = feat[at]
        return one_hot, (one_hot.astype(f32) * 128.0 - 128.0).astype(bf16)

    def attend(p, q_at, k_at):
        q, k, v = head_pair(qn, q_at, p), head_pair(kn, k_at, p), head_pair(vn, k_at, p)
        fq_, _ = masks(q_at)
        _, fk = masks(k_at)
        out = []
        for parity in range(2):
            mine = lambda a, b: jnp.where(low_head(a.shape) == (parity == 0), a, b)
            scores = dot_nt(mine(q, fq_), mine(k, fk))
            weights = jnp.exp(scores).astype(bf16)
            out.append(dot(weights, mine(v, jnp.ones_like(v))))
        return out

    def finish_attend(p, at, r0, r1):
        low = low_head(r0.shape)
        inverse = 1.0 / pltpu.roll(jnp.where(low, r1, r0), HD, 1)
        live = 1.0 - feat[at][:, pad_mark : pad_mark + 1].astype(f32)
        lane_at = pl.ds(pl.multiple_of(p * 128, 128), 128)
        inv[at, lane_at] = inverse
        o_all[c, at, lane_at] = (jnp.where(low, r0, r1) * inverse * live).astype(bf16)

    long_at, short_at = pl.ds(0, LONG), pl.ds(LONG, full - LONG)
    blocks = LONG // KB

    def block_at(b):
        return pl.ds(b * KB, KB)

    def steps_at(slot, p, b):
        for at in range(pairs):
            steps = plan(f"{slot}{at * blocks + b}")
            if steps:
                pl.when(p == at)(functools.partial(run, steps))

    def attend_pair(p):
        total = None
        for b in range(blocks):
            steps_at("F", p, b)
            if b == 0:
                project(p)
            parts = attend(p, long_at, block_at(b))
            if b < blocks - 1:
                for ref, part in zip((dkp, dvp), parts):
                    ref[long_at] = part if b == 0 else ref[long_at] + part
            else:
                total = [ref[long_at] + part for ref, part in zip((dkp, dvp), parts)]
        finish_attend(p, long_at, *total)
        finish_attend(p, short_at, *attend(p, short_at, short_at))

    loop(pairs, attend_pair)
    run(plan("OSEND"))
    send("o", o_all.at[c], o_all.at[c], sib)
    run(plan("OUT"))
    recv("wo", wo_other, sib)
    recv("o", o_all.at[nc], sib)

    def norm_parts(value, gain):
        centred = value - jnp.mean(value, axis=-1, keepdims=True)
        spread_ = jnp.mean(centred * centred, axis=-1, keepdims=True)
        scale = lax.rsqrt(spread_ + 1e-6)
        return centred * scale, scale

    step_rows = rows // 2

    def project_out(i):
        here = pl.ds(pl.multiple_of(i * step_rows, 64), step_rows)
        there = pl.ds(pl.multiple_of(c * rows + i * step_rows, 64), step_rows)
        o0, o1 = o_all[0, there], o_all[1, there]
        for j in range(2):
            cols = pl.ds(j * half, half)
            mixed = dot(o0, wo[j, pl.ds(0, half)]) + dot(o1, wo[j, pl.ds(half, half)])
            x1[here, cols] = xs[here, cols].astype(f32) + mixed
        normed, _ = norm_parts(x1[here], None)
        b_all[there] = (normed * gain_second).astype(bf16)

    for i in range(2):
        project_out(i)
        part = b_all.at[pl.ds(pl.multiple_of(c * rows + i * step_rows, 64), step_rows)]
        send(f"b{i}", part, part, sib)
    run(plan("PREH"))
    recv("yy", ys_sib, sib)
    for i in range(2):
        recv(f"b{i}", b_all.at[pl.ds(pl.multiple_of(nc * rows + i * step_rows, 64), step_rows)], sib)

    root = 0.7978845608028654

    def hidden(n):
        cols = pl.ds(pl.multiple_of(n * 512, 512), 512)
        zed = dot(b_all[...], wi[:, cols])
        square = zed * zed
        gate = 0.5 + 0.5 * jnp.tanh(zed * (root + (root * 0.044715) * square))
        activated = zed * gate
        slope = gate + (activated - activated * gate) * (2.0 * root + (6.0 * root * 0.044715) * square)
        activated = activated.astype(bf16)
        act[:, cols] = activated
        gp[:, cols] = slope.astype(bf16)
        gb[cols] = dot_tn(activated, ys[...]).astype(bf16)

    loop(ff // 512, hidden, plans("H", ff // 512))
    run(plan("DZ"))

    def hidden_back(n):
        cols = pl.ds(pl.multiple_of(n * 512, 512), 512)
        gp[:, cols] = (dot_nt(ys[...], wb[cols, :]) * gp[:, cols].astype(f32)).astype(bf16)

    loop(ff // 512, hidden_back)

    def tensor_sum(name, rows_of_sib, cols_of, landed):
        for n in range(width // 256):
            cols = pl.ds(n * 256, 256)
            tx[:, cols] = cols_of(rows_of_sib[...], n)
            send(f"{name}{n}", tx.at[:, cols], landed.at[:, cols], sib)

    def tensor_end(name, part, landed):
        for n in range(width // 256):
            cols = pl.ds(n * 256, 256)
            recv(f"{name}{n}", landed.at[:, cols], sib)
            landed[:, cols] = part[:, n * 256 : (n + 1) * 256] + landed[:, cols]

    def in_cols(rows_, n):
        return dot_nt(rows_, wi[pl.ds(n * 256, 256), :])

    def out_cols(rows_, n):
        return dot(rows_, wb[:, pl.ds(n * 256, 256)])

    for name in ("q", "o", "i"):
        wires.sent(f"{name}first", 2)
    run(plan("PI"))
    tensor_sum("pi", gp.at[sib_rows, :], in_cols, rx_b)

    def hidden_grad(n):
        cols = pl.ds(pl.multiple_of(n * 512, 512), 512)
        gi[:, cols] = dot_tn(b_all[...], gp[:, cols]).astype(bf16)

    run(plan("GI"))
    loop(ff // 512, hidden_grad)
    free_from, free_to = gains.at[1], gains_rx.at[1]
    send("free", free_from, free_to, sib)
    run(plan("PIEND"))
    tensor_end("pi", dot_nt(gp[own_rows, :], wi[...]), rx_b)

    ggrad[0] = jnp.zeros_like(ggrad[0])
    for i in range(2):
        wires.sent(f"b{i}")
    dxb = b_all

    def norm_back(grad, gain, normed, scale):
        lifted = grad * gain
        return scale * (
            lifted
            - jnp.mean(lifted, axis=-1, keepdims=True)
            - normed * jnp.mean(lifted * normed, axis=-1, keepdims=True)
        )

    def second_back(i):
        here = pl.ds(pl.multiple_of(i * 128, 128), 128)
        there = pl.ds(pl.multiple_of(c * rows + i * 128, 128), 128)
        grad = rx_b[here]
        normed, scale = norm_parts(x1[here], None)
        ggrad[0, 1:2, :] += jnp.sum(grad * normed, axis=0, keepdims=True)
        total = ys[there].astype(f32) + norm_back(grad, gain_second, normed, scale)
        rx_b[here] = total
        dxb[there] = total.astype(bf16)

    run(plan("SECOND"))
    loop(rows // 128, second_back)
    recv("free", free_to, sib)
    send("dx", dxb.at[own_rows], dxb.at[own_rows], sib)
    for n in range(width // 256):
        wires.sent(f"pi{n}")
    run(plan("PO"))
    tensor_sum("po", act.at[sib_rows, :], out_cols, rx_a)
    stages = [act.at[pl.ds(0, rows), pl.ds(3 * half, half)], gp.at[pl.ds(0, rows), pl.ds(3 * half, half)]]
    outs = [block_out.at[:, pl.ds(h * half, half)] for h in range(2)]
    at_b = wires.at("bo", 0, 2), wires.at("bo", 1, 2)

    ok_from, ok_to = gains.at[0], gains_rx.at[0]

    def finish_block():
        tensor_end("po", dot(act[own_rows, :], wb[...]), rx_a)
        for h in range(2):
            cols = pl.ds(h * half, half)
            stages[h][...] = (x1[:, cols] + rx_a[:, cols]).astype(bf16)
            wires.send_or_keep(swapped, at_b[0] + h, at_b[1] + h, stages[h], outs[h], outs[h], diag)
        send("ok", ok_from, ok_to, sib)

    do["finish"] = finish_block

    run(plan("GO"))
    recv("dx", dxb.at[sib_rows], sib)

    for j in range(2):
        go[pl.ds(j * half, half)] = dot_tn(o_all[j], dxb[:, head_rows]).astype(bf16)
    wires.sent("feat")
    run(plan("PB"))

    def project_back(i):
        at = pl.ds(pl.multiple_of(i * rows, 128), rows)
        grad = dot_nt(dxb[at, pl.ds(0, half)], wo[0, head_rows]) + dot_nt(
            dxb[at, pl.ds(half, half)], wo[1, head_rows]
        )
        live = 1.0 - feat[at][:, pad_mark : pad_mark + 1].astype(f32)
        do_all[at] = (grad.astype(bf16).astype(f32) * live * inv[at]).astype(bf16)

    loop(2, project_back)

    swap_heads = head_matrix(128, 1.0, True)

    def attend_back(p, q_at, k_at, first):
        q, k, v = head_pair(qn, q_at, p), head_pair(kn, k_at, p), head_pair(vn, k_at, p)
        grad = head_pair(do_all, q_at, p)
        lane_at = pl.ds(pl.multiple_of(p * 128, 128), 128)
        product = grad.astype(f32) * o_all[c, q_at, lane_at].astype(f32)
        delta = split_dot(product, swap_heads)
        d0 = delta.astype(bf16).astype(f32)
        d1 = (delta - d0).astype(bf16).astype(f32)
        d2 = delta - d0 - d1
        spot = lanes(delta.shape) % HD
        rider = jnp.where(spot == 0, -d0, jnp.where(spot == 1, -d1, jnp.where(spot == 2, -d2, 0.0))).astype(bf16)
        fq_, _ = masks(q_at)
        _, fk = masks(k_at)
        dqs, dks, dvs = [], [], []
        for parity in range(2):
            mine = lambda a, b: jnp.where(low_head(a.shape) == (parity == 0), a, b)
            weights = jnp.exp(dot_nt(mine(k, fk), mine(q, fq_)))
            slopes = dot_nt(mine(v, jnp.ones_like(v)), mine(grad, rider))
            dscores = (weights * slopes).astype(bf16)
            dvs.append(dot(weights.astype(bf16), grad))
            dks.append(dot(dscores, q))
            dqs.append(dot_tn(dscores, k))
        merge = lambda pair: jnp.where(low_head(pair[0].shape), pair[0], pair[1])
        dqp[q_at] = merge(dqs)
        for ref, parts in ((dkp, dks), (dvp, dvs)):
            ref[k_at] = merge(parts) if first else ref[k_at] + merge(parts)

    dproj = gp.at[:, pl.ds(0, 3 * half)]

    def head_back(p):
        lane_at = pl.ds(pl.multiple_of(p * 128, 128), 128)

        for i in range(2):
            at = pl.ds(i * rows, rows)
            for part, source, gain_row, scale_by in ((0, dqp, 2, HD**-0.5), (1, dkp, 3, 1.0)):
                lane_all = pl.ds(pl.multiple_of(c * half + p * 128, 128), 128)
                gain = gains[4, pl.ds(gain_row, 1), lane_all]
                centred = cen[at, pl.ds(pl.multiple_of(part * half + p * 128, 128), 128)].astype(f32)
                scale = lax.rsqrt(dot((centred * centred).astype(bf16), pair_mean) + 1e-6)
                normed = centred * scale
                grad = source[at] * scale_by if part == 0 else source[at]
                ggrad[0, pl.ds(gain_row, 1), lane_all] += jnp.sum(grad * normed, axis=0, keepdims=True)
                lifted = grad * gain
                back = scale * (
                    lifted - split_dot(lifted, pair_mean) - normed * split_dot(lifted * normed, pair_mean)
                )
                dproj[at, pl.ds(pl.multiple_of(p * pair_cols + part * 128, 128), 128)] = back.astype(bf16)
            dproj[at, pl.ds(pl.multiple_of(p * pair_cols + 256, 128), 128)] = dvp[at].astype(bf16)


    def weight_back(p):
        cols = pl.ds(pl.multiple_of(p * pair_cols, 128), pair_cols)
        act[pl.ds(0, width), cols] = dot_tn(a_all[...], dproj[:, cols]).astype(bf16)

    def back_pair(p):
        for b in range(blocks):
            steps_at("B", p, b)
            attend_back(p, block_at(b), long_at, b == 0)
        attend_back(p, short_at, short_at, True)
        head_back(p)
        weight_back(p)

    loop(pairs, back_pair)
    run(plan("PQ"))

    recv("ok", ok_to, sib)
    for n in range(width // 256):
        wires.sent(f"po{n}")

    def first_cols(rows_, n):
        return dot_nt(rows_, wq[pl.ds(n * 256, 256), :])

    tensor_sum("pq", dproj.at[sib_rows, :], first_cols, rx_a)
    run(plan("PQEND"))
    tensor_end("pq", dot_nt(dproj[own_rows, :], wq[...]), rx_a)
    run(plan("FIRST"))
    at_p = wires.at("pg", 0, rows // 128), wires.at("pg", 1, rows // 128)
    for i in range(rows // 128):
        here = pl.ds(i * 128, 128)
        grad = rx_a[here]
        normed, scale = norm_parts(xs[here].astype(f32), None)
        ggrad[0, 0:1, :] += jnp.sum(grad * normed, axis=0, keepdims=True)
        total = rx_b[here] + norm_back(grad, gain_first, normed, scale)
        xs[here] = total.astype(bf16)
        wires.send_or_keep(
            swapped, at_p[0] + i, at_p[1] + i, xs.at[here], patch_out.at[here], patch_out.at[here], diag
        )
    run(plan("END"))
    rest, mine = ggrad[4], None
    for _ in range(3):
        term = rest.astype(bf16)
        part = dot_nt(term, spread_gain)
        mine = part if mine is None else mine + part
        rest = rest - term.astype(f32)
    fg[...] = mine
    put_g = pltpu.make_async_copy(fg, gg_out, wires.recv_sems.at[wires.at("gout", 1)])
    put_g.start()
    outputs.append(put_g)
    for h in range(2):
        wires.recv_at(at_b[1] + h, outs[h], diag)
    for i in range(rows // 128):
        wires.recv_at(at_p[1] + i, patch_out.at[pl.ds(i * 128, 128)], diag)
    for put in outputs:
        put.wait()
    wires.drain()
    assert max(wires.sizes) <= SEMAPHORES


def run_layer(patches, cotangent, segments, weights, gain_rows):
    rows, width = patches.shape
    full = segments.shape[1]
    half = width // 2
    pairs = half // 128
    wq_in, wo_in, wi_in, wb_in = weights
    shard = wq_in.shape[0]
    nq, no, ni = wq_in.shape[1] // 2, wo_in.shape[1] // 2, wi_in.shape[1] // 2
    nb = wb_in.shape[1]
    depth, deep = 2 * shard, wb_in.shape[0]
    vm = lambda shape, kind=bf16: pltpu.VMEM(shape, kind)
    wide = (nq, no, ni)
    third = nq // pairs
    scratch = (
        [vm((rows, width)), vm((full, width)), vm((full, 128))]
        + [vm((width, nq)), vm((2, width, no)), vm((width, ni)), vm((SPAN * deep, nb))]
        + [vm((5, 8, width), f32), vm((7, 8, width), f32)]
        + [vm((full, width)), vm((full, width)), vm((full, half)), vm((full, half)), vm((full, half))]
        + [vm((2, full, half)), vm((full, half), f32), vm((rows, width), f32), vm((full, width))]
        + [vm((full, ni)), vm((full, ni))]
        + [vm((rows, width), f32)] * 3
        + [vm((full, half))]
        + [vm((full, 128), f32)] * 3
        + [vm((5, 8, width), f32), vm((7, 8, width), f32)]
        + [vm((width, no)), vm((width, ni)), vm((SPAN * deep, nb))]
    )
    for lead in ((NZ, 2), (NZ,), (NZ - 1,)):
        scratch += [vm((pairs, *lead, depth, third)), vm((*lead, depth, no)), vm((*lead, depth, ni)), vm((*lead, deep, nb))]
    scratch += [vm((pairs, 2, shard, third), f32), vm((2, shard, no), f32), vm((2, shard, ni), f32)] * 2
    scratch += [vm((deep, nb), f32), vm((8, shard), f32)]
    scratch += [pltpu.SemaphoreType.DMA((SEMAPHORES,)), pltpu.SemaphoreType.DMA((SEMAPHORES,))]
    here = pl.BlockSpec(memory_space=pltpu.VMEM)
    away = pl.BlockSpec(memory_space=pl.ANY)
    out = lambda shape, kind=f32: jax.ShapeDtypeStruct(shape, kind)
    return pl.pallas_call(
        layer_kernel,
        out_shape=(
            out((rows, width), bf16),
            out((rows, width), bf16),
            out((pairs, 2, shard, third)),
            out((2, shard, no)),
            out((2, shard, ni)),
            out((deep, nb)),
            out((8, shard)),
        ),
        in_specs=[away, away] + [here] * 6,
        out_specs=(away,) * 7,
        scratch_shapes=scratch,
        compiler_params=pltpu.CompilerParams(
            collective_id=0, has_side_effects=True, vmem_limit_bytes=VMEM_BYTES
        ),
        name="layer",
    )(patches, cotangent, segments, wq_in, wo_in, wi_in, wb_in, gain_rows)


def adam_step(weight, grad, first, second, rate, shrink):
    first_new = beta_one * first + (1.0 - beta_one) * grad
    second_new = beta_two * second + (1.0 - beta_two) * grad * grad
    first_fix = first_new / (1.0 - beta_one**STEP)
    second_fix = second_new / (1.0 - beta_two**STEP)
    weight_new = weight - rate * (first_fix / (jnp.sqrt(second_fix) + epsilon) + shrink * weight)
    return (first_new, second_new, weight_new)


def update_kernel(*refs):
    inputs, outs, held, news = refs[:22], refs[22:39], refs[39:59], refs[59:74]
    passing, (load_sems, store_sems, pass_sems) = refs[74:76], refs[76:]
    takes = [pltpu.make_async_copy(inputs[i], passing[i], pass_sems.at[i]) for i in range(2)]
    passes = [pltpu.make_async_copy(passing[i], outs[i], pass_sems.at[2 + i]) for i in range(2)]
    loads = [pltpu.make_async_copy(inputs[2 + i], held[i], load_sems.at[i]) for i in range(20)]
    stores = [pltpu.make_async_copy(news[i], outs[2 + i], store_sems.at[i]) for i in range(15)]
    order = (3, 2, 0, 1, 4)
    for at in order:
        for i in (at, 5 + at, 10 + at, 15 + at):
            loads[i].start()
    for copy in takes:
        copy.start()
    gq, go, gi, gb, gg = held[:5]
    state = held[5:]

    def update(at, cols, grad):
        weight, first, second = state[at], state[5 + at], state[10 + at]
        values = adam_step(weight[:, cols], grad, first[:, cols], second[:, cols], rate_list[at], shrink_list[at])
        for to, value in zip(news[3 * at : 3 * at + 3], values):
            to[:, cols] = value

    width = gb.shape[1]
    half = width // 2
    for at in order:
        for i in (at, 5 + at, 10 + at, 15 + at):
            loads[i].wait()
        if at == 0:
            for h in range(2):
                for part in range(3):
                    for p in range(half // 128):
                        grad = gq[p, h, :, pl.ds(part * 128, 128)]
                        update(0, pl.ds(part * width + h * half + p * 128, 128), grad)
        elif at == 1:
            for h in range(2):
                update(1, pl.ds(h * half, half), go[h])
        elif at == 2:
            group = gi.shape[2] // 8
            for pair in range(4):
                cols = pl.ds(2 * pair * group, 2 * group)
                first, second = gi[0, :, cols], gi[1, :, cols]
                low = lanes(first.shape) < group
                update(2, pl.ds(4 * pair * group, 2 * group), jnp.where(low, first, pltpu.roll(second, group, 1)))
                cols = pl.ds((4 * pair + 2) * group, 2 * group)
                update(2, cols, jnp.where(low, pltpu.roll(first, group, 1), second))
        elif at == 3:
            update(3, slice(None), gb[...])
        else:
            update(4, slice(None), gg[0:4, :])
        for i in range(3):
            stores[3 * at + i].start()
        if at == 3:
            for take, copy in zip(takes, passes):
                take.wait()
                copy.start()
    for copy in passes + stores:
        copy.wait()


def update_all(block, patch, grads, state):
    away = pl.BlockSpec(memory_space=pl.ANY)
    like = lambda v: jax.ShapeDtypeStruct(v.shape, v.dtype)
    news = tuple(like(state[i]) for i in range(5) for _ in range(3))
    operands = (*grads, *state)
    return pl.pallas_call(
        update_kernel,
        out_shape=(like(block), like(patch)) + news,
        in_specs=[away] * 22,
        out_specs=(away,) * 17,
        scratch_shapes=[pltpu.VMEM(v.shape, v.dtype) for v in operands]
        + [pltpu.VMEM(v.shape, v.dtype) for v in news]
        + [pltpu.VMEM(v.shape, v.dtype) for v in (block, patch)]
        + [pltpu.SemaphoreType.DMA((n,)) for n in (20, 15, 4)],
        compiler_params=pltpu.CompilerParams(vmem_limit_bytes=VMEM_BYTES),
        name="update",
    )(block, patch, *operands)


def shards(spans, patches, segments, cotangent, *state):
    dp, blk = lax.axis_index("dp"), lax.axis_index("blk")
    index = dp * 2 + blk
    members = 2 * SPAN
    place = index % members
    state = [v.T if i % 5 == 4 else v for i, v in enumerate(state)]
    weights = state[:5]

    def span_rows(weight, axis=0):
        if spans == 1:
            return weight
        whole = lax.all_gather(weight, ("dp", "blk"), axis=axis, tiled=True)
        depth = whole.shape[axis] // members
        return lax.dynamic_slice_in_dim(whole, place * depth, depth, axis)

    def span_sum(grad, rows, axis=0):
        shape = [n * members if i == axis else n for i, n in enumerate(grad.shape)]
        whole = lax.dynamic_update_slice_in_dim(jnp.zeros(shape, f32), grad, place * grad.shape[axis], axis)
        whole = lax.psum(whole, ("dp", "blk"))
        return lax.dynamic_slice_in_dim(whole, index * rows, rows, axis)

    block_out, patch_grad, *grads = run_layer(
        patches[0],
        cotangent[0],
        segments,
        [span_rows(w) for w in weights[:4]],
        span_rows(weights[4], 1),
    )
    if spans > 1:
        rows = [w.shape[0] for w in weights[:4]] + [weights[4].shape[1]]
        grads = [span_sum(g, n, axis) for g, n, axis in zip(grads, rows, (2, 1, 1, 0, 1))]
    block_out, patch_grad, *news = update_all(block_out, patch_grad, grads, state)
    news = [v.T if i >= 12 else v for i, v in enumerate(news)]
    return (block_out[None], patch_grad[None], *news)


def solution(mesh):
    rows, tokens = P(("dp", "blk"), None), P("dp", "blk", None)
    return jax.shard_map(
        functools.partial(shards, mesh.shape["dp"] // SPAN),
        mesh=mesh,
        in_specs=(tokens, P("dp", None), tokens) + (rows,) * 15,
        out_specs=(tokens, tokens) + (rows,) * 15,
        check_vma=False,
    )
```

```python
import functools

import jax
import jax.numpy as jnp
from jax import lax
from jax.experimental import pallas as pl
from jax.experimental.pallas import tpu as pltpu
from jax.sharding import PartitionSpec as P

H = 12
HD = 64
STEP = 5
SPAN = 16
NZ = 4

pad_mark = 7
beta_one = 0.5
beta_two = 0.5
epsilon = 1e-08
rate_list = (0.03, 0.1, 0.03, 0.02, 0.1)
shrink_list = (0.1, 0.1, 0.1, 0.1, 0.0)

MESH = pl.DeviceIdType.MESH
f32 = jnp.float32
bf16 = jnp.bfloat16
LONG = 1024
KB = 512
PLAN = {
    "LN1": (115, 121, 116, 99, 117, 118, 122, 0, 125, 1, 100, 101, 16, 120, 119, 49, 84, 102, 17, 32, 22, 4, 103, 127, 7, 5, 48, 65, 20, 37, 104, 6, 105, 64, 9, 38, 54, 55, 106,),
    "F0": (33, 52, 36, 10, 21, 8, 24, 26, 83, 128, 56, 71, 53, 123, 25, 2, 23, 58,),
    "F1": (39, 41,),
    "F2": (57, 18, 42, 40, 68, 69,),
    "F3": (87, 50, 34,),
    "F4": (124, 70,),
    "F5": (89,),
    "OSEND": (72,),
    "OUT": (73, 74, 126,),
    "PREH": (91,),
    "H0": (90, 93, 88, 66,),
    "H1": (92,),
    "DZ": (86, 85,),
    "SECOND": (96,),
    "PO": (67, 94, 95,),
    "B1": (51, 140,),
    "B2": (3, 76,),
    "B3": (142, 141, 62, 59, 61, 60,),
    "B4": (19, 14, 11, 75, 13, 77, 12, 78, 80,),
    "PQ": (63, 15, 27,),
    "PQEND": (35, 79, 28, 133, 29, 30, 97, 98, 131,),
    "END": (107, 144, 147, 143, 145, 146, 46, 134, 108, 81, 45, 109, 132, 82, 110, 31, 43, 111, 139, 44, 112, 129, 47, 113, 135, 137, 114, 136, 130, 138,),
}
VMEM_BYTES = 66 * 2**20 - 2**19
SEND_SEMAPHORES, RECV_SEMAPHORES = 64, 152


def dot(a, b):
    return lax.dot_general(a, b, (((1,), (0,)), ((), ())), preferred_element_type=f32)


def dot_nt(a, b):
    return lax.dot_general(a, b, (((1,), (1,)), ((), ())), preferred_element_type=f32)


def dot_tn(a, b):
    return lax.dot_general(a, b, (((0,), (0,)), ((), ())), preferred_element_type=f32)


def split_dot(value, matrix):
    high = value.astype(bf16)
    rest = (value - high.astype(f32)).astype(bf16)
    return dot(high, matrix) + dot(rest, matrix)


def lanes(shape):
    return lax.broadcasted_iota(jnp.int32, shape, len(shape) - 1)


def head_matrix(width, scale, swap):
    row = lax.broadcasted_iota(jnp.int32, (width, width), 0) // HD
    col = lax.broadcasted_iota(jnp.int32, (width, width), 1) // HD
    if swap:
        col = col + 1 - 2 * (col % 2)
    return jnp.where(row == col, scale, 0.0).astype(bf16)


def loop(count, body, before=()):
    def one(i, carry):
        for at, steps in enumerate(before):
            if steps:
                pl.when(i == at)(functools.partial(run, steps))
        body(i)
        return carry

    lax.fori_loop(0, count, one, 0)


def run(steps):
    for step in steps:
        step()


class Wires:
    def __init__(self, send_sems, recv_sems):
        self.send_sems, self.recv_sems = send_sems, recv_sems
        self.names = {}
        self.sizes = [0, 0]
        self.pending = {}

    def at(self, name, side, count=1):
        if (name, side) not in self.names:
            self.names[name, side] = self.sizes[side]
            self.sizes[side] += count
        return self.names[name, side]

    def make(self, send_at, recv_at, src, dst, dev):
        return pltpu.make_async_remote_copy(
            src_ref=src,
            dst_ref=dst,
            send_sem=self.send_sems.at[send_at],
            recv_sem=self.recv_sems.at[recv_at],
            device_id=dev,
            device_id_type=MESH,
        )

    def send(self, name, src, dst, dev):
        self.send_at(self.at(name, 0), self.at(name, 1), src, dst, dev)

    def send_at(self, send_at, recv_at, src, dst, dev):
        self.make(send_at, recv_at, src, dst, dev).start()
        self.pending[send_at] = lambda: self.make(send_at, 0, src, src, dev).wait_send()

    def send_group(self, group, whole, name, src, dst, dev):
        send_at = self.at(group, 0)
        self.make(send_at, self.at(name, 1), src, dst, dev).start()
        self.pending[send_at] = lambda: self.make(send_at, 0, whole, whole, dev).wait_send()

    def recv(self, name, dst, dev):
        self.recv_at(self.at(name, 1), dst, dev)

    def recv_at(self, at, dst, dev):
        self.make(0, at, dst, dst, dev).wait_recv()

    def send_or_keep(self, remote, send_at, recv_at, src, dst, kept, dev):
        def far():
            self.make(send_at, recv_at, src, dst, dev).start()

        def near():
            pltpu.make_async_copy(src, kept, self.recv_sems.at[recv_at]).start()

        pl.when(remote)(far)
        pl.when(jnp.logical_not(remote))(near)

        def finish():
            pl.when(remote)(lambda: self.make(send_at, 0, src, dst, dev).wait_send())

        self.pending[send_at] = finish

    def sent(self, name, count=1):
        for i in range(count):
            self.pending.pop(self.at(name, 0) + i)()

    def drain(self):
        for finish in self.pending.values():
            finish()
        self.pending = {}


def layer_kernel(
    patch_in, cot_in, seg_in, wq_in, wo_in, wi_in, wb_in, gain_in,
    block_out, patch_out, gq_out, go_out, gi_out, gb_out, gg_out,
    xs, ys, feat, wq, wo, wi, wb, gains, gains_rx,
    a_all, cen, qn, kn, vn, o_all, inv, x1, b_all, act, gp, tx, rx_a, rx_b,
    do_all, dqp, dkp, dvp, ggrad, ggrad_rx,
    go, gi, gb, r1q, r1o, r1i, r1b, r2q, r2o, r2i, r2b, r3q, r3o, r3i, r3b,
    fq, fo, fi, uq, uo, ui, fb, fg,
    send_sems, recv_sems,
):
    rows, width = xs.shape
    full = a_all.shape[0]
    half = width // 2
    ff = wi.shape[1]
    pairs = half // 128
    dp, y = lax.axis_index("dp"), lax.axis_index("blk")
    base = dp // SPAN * SPAN
    z, x, c = dp % SPAN // 4, dp % 4 // 2, dp % 2
    ny, nx, nc = 1 - y, 1 - x, 1 - c
    swapped = c != y

    def dev(z_, x_, c_, y_):
        return (base + (z_ * 2 + x_) * 2 + c_, y_)

    sib = dev(z, x, nc, y)
    ynb = dev(z, x, c, ny)
    xnb = dev(z, nx, c, y)
    diag = dev(z, x, nc, ny)
    zs = [dev((z + d) % NZ, x, c, y) for d in range(NZ)]
    wires = Wires(send_sems, recv_sems)
    send, recv = wires.send, wires.recv

    barrier = pltpu.get_barrier_semaphore()
    partners = [sib, ynb, xnb, diag] + zs[1:]
    for partner in partners:
        pl.semaphore_signal(barrier, inc=1, device_id=partner, device_id_type=MESH)

    own_rows = pl.ds(pl.multiple_of(c * rows, 128), rows)
    sib_rows = pl.ds(pl.multiple_of(nc * rows, 128), rows)
    head_rows = pl.ds(pl.multiple_of(c * half, 128), half)

    def block(z_, x_, y_):
        return (z_ * 2 + x_) * 2 + y_

    def turns(o):
        no = 1 - o
        return x + o - 2 * x * o, y + no - 2 * y * no, x + no - 2 * x * no, y + o - 2 * y * o

    class Matrix:
        def __init__(self, name, weight, grad, buffers, order, early, back_order, back_early):
            first, second, third = buffers
            self.name = name
            self.early, self.back_early = early, back_early
            self.rx2_three = second.at[pl.ds(0, 3)]
            self.rx1 = [[first.at[d, r] for r in range(2)] for d in range(NZ)]
            self.rx1_both = [first.at[d] for d in range(NZ)]
            self.rx2 = [second.at[d] for d in range(NZ)]
            self.rx3 = [third.at[d] for d in range(NZ - 1)]
            self.rx3_all = third
            self.depth = weight.shape[0] // SPAN
            self.sent_weight = weight.at[pl.ds(0, 15 * self.depth)]
            self.sent_grad = grad.at[pl.ds(0, 15 * self.depth)]
            self.last_weight = weight.at[pl.ds(0, 8 * self.depth)]
            xf, yf, xs_, ys_ = turns(order)
            self.near, self.next = dev(z, xf, c, yf), dev(z, xs_, c, ys_)
            back = [(z + NZ - d) % NZ for d in range(NZ)]
            ahead = [(z + d) % NZ for d in range(NZ)]
            self.at_z = [self.at(weight, block(zd, x, y)) for zd in back]
            self.at_near = [self.at(weight, block(zd, xf, yf)) for zd in back]
            xf, yf, xs_, ys_ = turns(back_order)
            self.back_near, self.back_next = dev(z, xf, c, yf), dev(z, xs_, c, ys_)
            self.to_next = [[self.at(grad, block(zd, xs_, ys_)), self.at(grad, block(zd, nx, ny))] for zd in ahead]
            self.to_near = [self.at(grad, block(zd, xf, yf)) for zd in ahead]
            self.to_z = [self.at(grad, block(zd, x, y)) for zd in ahead]

        def at(self, ref, b):
            return ref.at[pl.ds(pl.multiple_of(b * self.depth, 16), self.depth)]

        def pass_on(self, name, piece, to):
            wires.send_group(f"{self.name}g", self.sent_weight, f"{self.name}{name}", piece, piece, to)

        def gather_own_z(self):
            for d in range(1, NZ):
                self.pass_on(f"z{d}", self.at_z[0], zs[d])

        def gather_own_near(self):
            self.pass_on("f0", self.at_z[0], self.near)
            self.pass_on("s", self.at_z[0], self.next)

        def gather_own(self):
            self.gather_own_z()
            self.gather_own_near()

        def gather_z(self, d):
            recv(f"{self.name}z{d}", self.at_z[d], zs[1])
            if not self.early:
                self.pass_on(f"f{d}", self.at_z[d], self.near)
            self.pass_on("s", self.at_z[d], self.next)

        def gather_near(self, d):
            recv(f"{self.name}f{d}", self.at_near[d], self.near)
            if self.early and d == 0:
                for k in range(1, NZ):
                    self.pass_on(f"f{k}", self.at_near[0], zs[k])
            self.pass_on("s", self.at_near[d], self.next)

        def gather_end(self):
            recv(f"{self.name}s", self.last_weight, self.next)

        def gather_steps(self):
            from_z = [functools.partial(self.gather_z, d) for d in (1, 2, 3)]
            from_near = [functools.partial(self.gather_near, d) for d in (0, 1, 2, 3)]
            return from_near[:1] + from_z + from_near[1:] if self.early else from_z + from_near

        def back(self, name, piece, landed, to):
            wires.send_group(f"{self.name}r", self.sent_grad, f"{self.name}{name}", piece, landed, to)

        def reduce_start(self):
            for d in (1, 2, 3, 0):
                for r in (1, 0):
                    self.back(f"a{d}", self.to_next[d][r], self.rx1[d][r], self.back_next)

        def add(self, piece, landed):
            def some(i):
                at = pl.ds(pl.multiple_of(i * 16, 16), 16)
                piece[at] = (piece[at].astype(f32) + landed[at].astype(f32)).astype(bf16)

            loop(self.depth // 16, some)

        def reduce_next(self, d):
            recv(f"{self.name}a{d}", self.rx1_both[d], self.back_next)
            self.add(self.to_near[d], self.rx1[d][1])
            if not self.back_early:
                self.back(f"b{d}", self.to_near[d], self.rx2[d], self.back_near)
            elif d:
                self.back("e", self.to_near[d], self.rx2[d - 1], zs[d])
            self.add(self.to_z[d], self.rx1[d][0])
            if self.back_early and d:
                self.back("c", self.to_z[d], self.rx3[d - 1], zs[d])

        def reduce_near(self, d):
            recv(f"{self.name}b{d}", self.rx2[d], self.back_near)
            self.add(self.to_z[d], self.rx2[d])
            if d:
                self.back("c", self.to_z[d], self.rx3[d - 1], zs[d])

        def reduce_near_early(self):
            recv(f"{self.name}e", self.rx2_three, zs[1])
            total = self.to_near[0][...].astype(f32)
            for landed in self.rx2[:3]:
                total = total + landed[...].astype(f32)
            self.to_near[0][...] = total.astype(bf16)
            self.back("n", self.to_near[0], self.rx2[3], self.back_near)

        def reduce_end(self):
            recv(f"{self.name}c", self.rx3_all, zs[1])
            total = self.to_z[0][...].astype(f32)
            for landed in self.rx3:
                total = total + landed[...].astype(f32)
            if self.back_early:
                recv(f"{self.name}n", self.rx2[3], self.back_near)
                total = total + self.rx2[3][...].astype(f32)
            return total

        def reduce_steps(self):
            first = [functools.partial(self.reduce_next, d) for d in (1, 2, 3, 0)]
            if self.back_early:
                return first, [self.reduce_near_early]
            return first, [functools.partial(self.reduce_near, d) for d in (1, 2, 3, 0)]

    pair_cols = 3 * 128
    gq = [act.at[pl.ds(0, width), pl.ds(p * pair_cols, pair_cols)] for p in range(pairs)]
    mq = [
        Matrix(
            f"q{p}", wq.at[:, pl.ds(p * pair_cols, pair_cols)], gq[p], (r1q.at[p], r2q.at[p], r3q.at[p]), 0, False, c, True
        )
        for p in range(pairs)
    ]
    mo = Matrix("o", wo.at[c], go, (r1o, r2o, r3o), 0, False, 0, True)
    mi = Matrix("i", wi, gi, (r1i, r2i, r3i), c, True, c, False)
    mb = Matrix("b", wb, gb, (r1b, r2b, r3b), c, False, c, True)

    padded = -(-wq_in.shape[0] // 16) * 16

    def pieces(at, cols):
        return lambda h: gi.at[pl.ds(pl.multiple_of((2 * at + h) * padded, 16), padded), pl.ds(0, cols)]

    sq, rq = pieces(0, wq.shape[1]), pieces(1, wq.shape[1])
    so, ro = pieces(2, half), pieces(3, half)
    si, ri = pieces(4, ff), pieces(5, ff)

    def spread(name, staged, landed):
        to, at = wires.at(f"{name}first", 1, 2) + y, wires.at(f"{name}first", 0, 2)
        other, same, slot = staged(nc), staged(c), landed(y)
        far, near = dev(z, x, nc, c), dev(z, x, c, c)

        def go_on():
            wires.send_at(at, to, other, slot, far)
            wires.send_or_keep(swapped, at + 1, to, same, slot, slot, near)

        return go_on

    def collect(name, landed, *fills):
        at = wires.at(f"{name}first", 1, 2)
        slots = [landed(p) for p in range(2)]

        def go_on():
            for p in range(2):
                wires.recv_at(at + p, slots[p], sib)
            for matrix, cols in fills:
                fill(slots, matrix, cols)

        return go_on

    def fill(slots, matrix, cols):
        parts = [slot[:, cols].astype(f32)[: matrix.depth // 2] for slot in slots]
        matrix.at_z[0][...] = jnp.concatenate(parts, 0).astype(bf16)

    def unspread(name, matrix, ready, landed):
        to, at = wires.at(f"{name}last", 1, 2), wires.at(f"{name}last", 0, 2)
        far, near = dev(z, x, y, ny), dev(z, x, y, y)
        depth = matrix.depth // 2
        slot_at = to + c
        other, same, slot = ready.at[ny], ready.at[y], landed.at[c]

        def go_on():
            total = matrix.reduce_end()
            for p in range(2):
                ready[p] = total[p * depth : (p + 1) * depth]
            wires.send_at(at, slot_at, other, slot, far)
            wires.send_or_keep(swapped, at + 1, slot_at, same, slot, slot, near)

        return go_on

    def unspread_end(name, landed, out):
        at = wires.at(f"{name}last", 1, 2)
        slots = [landed.at[p] for p in range(2)]
        put = pltpu.make_async_copy(landed, out, wires.recv_sems.at[wires.at(f"{name}out", 1)])
        outputs.append(put)

        def go_on():
            for p in range(2):
                wires.recv_at(at + p, slots[p], sib)
            put.start()

        return go_on

    outputs = []

    def sum_hops(name, own, landed, order):
        own, landed = [own.at[k] for k in range(5)], [landed.at[k] for k in range(7)]

        def one(k, partner):
            def start():
                send(f"{name}{k}", own[k], landed[k], partner)

            def end():
                recv(f"{name}{k}", landed[k], partner)
                own[k + 1][...] = own[k][...] + landed[k][...]

            return start, end

        def along_z(k):
            def start():
                for d in range(1, NZ):
                    send(f"{name}z{d}", own[k], landed[3 + d], zs[d])

            def end():
                total = own[k][...]
                for d in range(1, NZ):
                    recv(f"{name}z{d}", landed[3 + d], zs[1])
                    total = total + landed[3 + d][...]
                own[k + 1][...] = total

            return start, end

        return [along_z(k) if who is None else one(k, who) for k, who in enumerate(order)]

    def place_lanes(depth):
        row = lax.broadcasted_iota(jnp.int32, (depth, width), 0)
        spot = ((z * 2 + x) * 2 + c) * 2 + y
        return lanes((depth, width)) == row + spot * depth

    feat_own, feat_rx = do_all.at[:, pl.ds(0, 128)], do_all.at[:, pl.ds(128, 128)]
    gains[0] = jnp.zeros_like(gains[0])
    spread_gain = jnp.where(place_lanes(gain_in.shape[1]), 1.0, 0.0).astype(bf16)
    gains[0, 0:4, :] = dot(gain_in[...].astype(bf16), spread_gain)
    seg_lane = lax.broadcasted_iota(jnp.int32, (128, full), 0) % HD
    feat_own[...] = jnp.where(seg_lane == seg_in[...], 1.0, 0.0).astype(bf16).T
    depth = wq_in.shape[0]
    pad = jnp.zeros((padded - depth, 128), f32)
    for h in range(2):
        for p in range(pairs):
            for part in range(3):
                take = wq_in[:, pl.ds(part * width + h * half + p * 128, 128)]
                sq(h)[:, pl.ds(p * pair_cols + part * 128, 128)] = jnp.concatenate([take, pad], 0).astype(bf16)
    def prepare():
        pad = jnp.zeros((padded - depth, half), f32)
        for h in range(2):
            so(h)[...] = jnp.concatenate([wo_in[:, pl.ds(h * half, half)], pad], 0).astype(bf16)
        group = ff // 8
        pad = jnp.zeros((padded - depth, 2 * group), f32)
        for pair in range(4):
            even = wi_in[:, pl.ds(4 * pair * group, 2 * group)]
            odd = wi_in[:, pl.ds((4 * pair + 2) * group, 2 * group)]
            low_lane = lanes(even.shape) < group
            first = jnp.where(low_lane, even, pltpu.roll(odd, group, 1))
            second = jnp.where(low_lane, pltpu.roll(even, group, 1), odd)
            for h, value in enumerate((first, second)):
                si(h)[:, pl.ds(2 * pair * group, 2 * group)] = jnp.concatenate([value, pad], 0).astype(bf16)
        mb.at_z[0][...] = wb_in[...].astype(bf16)

    do = {}

    def plan(slot):
        steps = list(do.values())
        return [steps[k] for k in PLAN.get(slot, ())]

    def plans(slot, count):
        return [plan(f"{slot}{t}") for t in range(count)]

    for matrix in (*mq, mo, mi, mb):
        name = matrix.name
        do[f"{name}z"], do[f"{name}n"] = matrix.gather_own_z, matrix.gather_own_near
        do[f"{name}.end"], do[f"{name}.rs"] = matrix.gather_end, matrix.reduce_start
        first_steps, rest_steps = matrix.reduce_steps()
        for kind, steps in (("g", matrix.gather_steps()), ("a", first_steps), ("r", rest_steps)):
            for k, step in enumerate(steps):
                do[f"{name}.{kind}{k}"] = step
    for prefix, hops, keys in (
        ("", sum_hops("gain", gains, gains_rx, (ynb, None, xnb, sib)), "yzxs"),
        ("t", sum_hops("gg", ggrad, ggrad_rx, (ynb, sib, xnb, None)), "ysxz"),
    ):
        for key, (start, end) in zip(keys, hops):
            do[f"{prefix}h{key}0"], do[f"{prefix}h{key}1"] = start, end
    all_cols = slice(None)
    do["sq"], do["so"], do["si"] = spread("q", sq, rq), spread("o", so, ro), spread("i", si, ri)
    do["cq"] = collect("q", rq, *[(mq[p], pl.ds(p * pair_cols, pair_cols)) for p in range(pairs)])
    do["co"], do["ci"] = collect("o", ro, (mo, all_cols)), collect("i", ri, (mi, all_cols))
    do["prep"] = prepare
    xs_at, ys_at = (wires.at("xs", 0), wires.at("xs", 1)), (wires.at("ys", 0), wires.at("ys", 1))
    ys_own, ys_sib, wo_mine, wo_other = ys.at[own_rows], ys.at[sib_rows], wo.at[c], wo.at[nc]
    do["xs"] = lambda: wires.send_or_keep(swapped, *xs_at, patch_in, xs, xs, diag)
    do["ys"] = lambda: wires.send_or_keep(swapped, *ys_at, cot_in, ys_sib, ys_own, diag)
    do["share"] = lambda: send("wo", wo_mine, wo_mine, sib)
    do["feat"] = lambda: send("feat", feat_own, feat_rx, sib)

    def pass_cotangent():
        wires.recv_at(ys_at[1], ys_own, diag)
        send("yy", ys_own, ys_own, sib)

    def pick_feat():
        recv("feat", feat_rx, sib)
        feat[...] = jnp.where(swapped, feat_rx[...], feat_own[...])

    a_sib = a_all.at[sib_rows]
    do["ysr"], do["featr"] = pass_cotangent, pick_feat
    do["ar"] = lambda: recv("a", a_sib, sib)
    ends = [("i", mi, fi, ui, gi_out), ("o", mo, fo, uo, go_out)]
    ends += [(f"q{p}", mq[p], fq.at[p], uq.at[p], gq_out.at[p]) for p in range(pairs)]
    for name, matrix, ready, landed, out in ends:
        do[f"{name}.e"] = unspread(name, matrix, ready, landed)
        do[f"{name}.p"] = unspread_end(name, landed, out)
    put_b = pltpu.make_async_copy(fb, gb_out, wires.recv_sems.at[wires.at("bout", 1)])
    outputs.append(put_b)

    def end_b():
        fb[...] = mb.reduce_end()
        put_b.start()

    do["b.e"] = end_b

    pl.semaphore_wait(barrier, len(partners))
    run(plan("LN1"))
    gain_first, gain_second = gains[4, 0:1, :], gains[4, 1:2, :]
    wires.recv_at(xs_at[1], xs, diag)

    def norm_one(i):
        v = xs[pl.ds(pl.multiple_of(i * 128, 128), 128)].astype(f32)
        centred = v - jnp.mean(v, axis=-1, keepdims=True)
        spread_ = jnp.mean(centred * centred, axis=-1, keepdims=True)
        normed = centred * lax.rsqrt(spread_ + 1e-6) * gain_first
        a_all[pl.ds(pl.multiple_of(c * rows + i * 128, 128), 128)] = normed.astype(bf16)

    loop(rows // 128, norm_one)
    send("a", a_all.at[own_rows], a_all.at[own_rows], sib)
    pair_mean = head_matrix(128, 1.0 / HD, False)

    def project(p):
        lane_at = pl.ds(pl.multiple_of(p * 128, 128), 128)
        lane_all = pl.ds(pl.multiple_of(c * half + p * 128, 128), 128)

        def some(i):
            at = pl.ds(pl.multiple_of(i * rows, 128), rows)
            projected = dot(a_all[at], wq[:, pl.ds(pl.multiple_of(p * pair_cols, 128), pair_cols)])
            for part, to in ((0, qn), (1, kn)):
                value = projected[:, part * 128 : (part + 1) * 128]
                centred = value - split_dot(value, pair_mean)
                spread_ = dot((centred * centred).astype(bf16), pair_mean)
                cen[at, pl.ds(pl.multiple_of(part * half + p * 128, 128), 128)] = centred.astype(bf16)
                normed = (centred * lax.rsqrt(spread_ + 1e-6) * gains[4, pl.ds(2 + part, 1), lane_all]).astype(bf16)
                to[at, lane_at] = normed * (HD**-0.5) if part == 0 else normed
            vn[at, lane_at] = projected[:, 256:].astype(bf16)

        loop(2, some)

    low_head = lambda shape: lanes(shape) < HD

    def head_pair(ref, at, p):
        return ref[at, pl.ds(pl.multiple_of(p * 128, 128), 128)]

    def masks(at):
        one_hot = feat[at]
        return one_hot, (one_hot.astype(f32) * 128.0 - 128.0).astype(bf16)

    def attend(p, q_at, k_at):
        q, k, v = head_pair(qn, q_at, p), head_pair(kn, k_at, p), head_pair(vn, k_at, p)
        fq_, _ = masks(q_at)
        _, fk = masks(k_at)
        out = []
        for parity in range(2):
            mine = lambda a, b: jnp.where(low_head(a.shape) == (parity == 0), a, b)
            scores = dot_nt(mine(q, fq_), mine(k, fk))
            weights = jnp.exp(scores).astype(bf16)
            out.append(dot(weights, mine(v, jnp.ones_like(v))))
        return out

    def finish_attend(p, at, r0, r1):
        low = low_head(r0.shape)
        inverse = 1.0 / pltpu.roll(jnp.where(low, r1, r0), HD, 1)
        live = 1.0 - feat[at][:, pad_mark : pad_mark + 1].astype(f32)
        lane_at = pl.ds(pl.multiple_of(p * 128, 128), 128)
        inv[at, lane_at] = inverse
        o_all[c, at, lane_at] = (jnp.where(low, r0, r1) * inverse * live).astype(bf16)

    long_at, short_at = pl.ds(0, LONG), pl.ds(LONG, full - LONG)
    blocks = LONG // KB

    def block_at(b):
        return pl.ds(b * KB, KB)

    def steps_at(slot, p, b):
        for at in range(pairs):
            steps = plan(f"{slot}{at * blocks + b}")
            if steps:
                pl.when(p == at)(functools.partial(run, steps))

    def attend_step(t):
        p, b = t // blocks, t % blocks
        pl.when(b == 0)(lambda: project(p))
        parts = attend(p, long_at, pl.ds(pl.multiple_of(b * KB, KB), KB))

        @pl.when(b == 0)
        def _():
            for ref, part in zip((dkp, dvp), parts):
                ref[long_at] = part

        @pl.when(b > 0)
        def _():
            for ref, part in zip((dkp, dvp), parts):
                ref[long_at] += part

        @pl.when(b == blocks - 1)
        def _():
            finish_attend(p, long_at, dkp[long_at], dvp[long_at])
            finish_attend(p, short_at, *attend(p, short_at, short_at))

    loop(pairs * blocks, attend_step, plans("F", pairs * blocks))
    run(plan("OSEND"))
    send("o", o_all.at[c], o_all.at[c], sib)
    run(plan("OUT"))
    recv("wo", wo_other, sib)
    recv("o", o_all.at[nc], sib)

    def norm_parts(value, gain):
        centred = value - jnp.mean(value, axis=-1, keepdims=True)
        spread_ = jnp.mean(centred * centred, axis=-1, keepdims=True)
        scale = lax.rsqrt(spread_ + 1e-6)
        return centred * scale, scale

    step_rows = rows // 2

    def project_out(i):
        here = pl.ds(pl.multiple_of(i * step_rows, 64), step_rows)
        there = pl.ds(pl.multiple_of(c * rows + i * step_rows, 64), step_rows)
        o0, o1 = o_all[0, there], o_all[1, there]
        for j in range(2):
            cols = pl.ds(j * half, half)
            mixed = dot(o0, wo[j, pl.ds(0, half)]) + dot(o1, wo[j, pl.ds(half, half)])
            x1[here, cols] = xs[here, cols].astype(f32) + mixed
        normed, _ = norm_parts(x1[here], None)
        b_all[there] = (normed * gain_second).astype(bf16)

    for i in range(2):
        project_out(i)
        part = b_all.at[pl.ds(pl.multiple_of(c * rows + i * step_rows, 64), step_rows)]
        send(f"b{i}", part, part, sib)
    run(plan("PREH"))
    recv("yy", ys_sib, sib)
    for i in range(2):
        recv(f"b{i}", b_all.at[pl.ds(pl.multiple_of(nc * rows + i * step_rows, 64), step_rows)], sib)

    root = 0.7978845608028654

    def hidden(n):
        at = pl.ds(pl.multiple_of(n * 256, 256), 256)
        zed = dot(b_all[at], wi[...])
        square = zed * zed
        gate = 0.5 + 0.5 * jnp.tanh(zed * (root + (root * 0.044715) * square))
        activated = zed * gate
        slope = gate + (activated - activated * gate) * (2.0 * root + (6.0 * root * 0.044715) * square)
        act[at] = activated.astype(bf16)
        gp[at] = slope.astype(bf16)

    loop(full // 256, hidden, [plan("H0")] + [()] * (full // 256 - 1))

    def back_grad(n):
        cols = pl.ds(pl.multiple_of(n * 512, 512), 512)
        gb[cols] = dot_tn(act[:, cols], ys[...]).astype(bf16)

    loop(ff // 512, back_grad, [plan("H1"), plan("H2"), ()])
    run(plan("DZ"))

    def hidden_back(n):
        cols = pl.ds(pl.multiple_of(n * 512, 512), 512)
        gp[:, cols] = (dot_nt(ys[...], wb[cols, :]) * gp[:, cols].astype(f32)).astype(bf16)

    loop(ff // 512, hidden_back)

    def tensor_sum(name, rows_of_sib, cols_of, landed, cuts):
        for n, cut in enumerate(zip(cuts, cuts[1:])):
            cols = pl.ds(cut[0], cut[1] - cut[0])
            tx[:, cols] = cols_of(rows_of_sib[...], cols)
            send(f"{name}{n}", tx.at[:, cols], landed.at[:, cols], sib)

    def tensor_end(name, part, landed, cuts):
        for n, cut in enumerate(zip(cuts, cuts[1:])):
            cols = pl.ds(cut[0], cut[1] - cut[0])
            recv(f"{name}{n}", landed.at[:, cols], sib)
        for r in range(0, rows, 128):
            landed[r : r + 128] = part[r : r + 128] + landed[r : r + 128]

    whole_cut, two_cuts = (0, width), (0, width - 256, width)

    def in_cols(rows_, cols):
        return dot_nt(rows_, wi[cols, :])

    def out_cols(rows_, cols):
        return dot(rows_, wb[:, cols])

    for name in ("q", "o", "i"):
        wires.sent(f"{name}first", 2)
    run(plan("PI"))
    tensor_sum("pi", gp.at[sib_rows, :], in_cols, rx_b, whole_cut)

    def hidden_grad(n):
        cols = pl.ds(pl.multiple_of(n * 512, 512), 512)
        gi[:, cols] = dot_tn(b_all[...], gp[:, cols]).astype(bf16)

    run(plan("GI"))
    loop(ff // 512, hidden_grad)
    free_from, free_to = gains.at[1], gains_rx.at[1]
    send("free", free_from, free_to, sib)
    run(plan("PIEND"))
    tensor_end("pi", dot_nt(gp[own_rows, :], wi[...]), rx_b, whole_cut)

    ggrad[0] = jnp.zeros_like(ggrad[0])
    for i in range(2):
        wires.sent(f"b{i}")
    dxb = b_all

    def norm_back(grad, gain, normed, scale):
        lifted = grad * gain
        return scale * (
            lifted
            - jnp.mean(lifted, axis=-1, keepdims=True)
            - normed * jnp.mean(lifted * normed, axis=-1, keepdims=True)
        )

    def second_back(i):
        here = pl.ds(pl.multiple_of(i * 128, 128), 128)
        there = pl.ds(pl.multiple_of(c * rows + i * 128, 128), 128)
        grad = rx_b[here]
        normed, scale = norm_parts(x1[here], None)
        ggrad[0, 1:2, :] += jnp.sum(grad * normed, axis=0, keepdims=True)
        total = ys[there].astype(f32) + norm_back(grad, gain_second, normed, scale)
        rx_b[here] = total
        dxb[there] = total.astype(bf16)

    run(plan("SECOND"))
    loop(rows // 128, second_back)
    recv("free", free_to, sib)
    send("dx", dxb.at[own_rows], dxb.at[own_rows], sib)
    wires.sent("pi0")
    run(plan("PO"))
    tensor_sum("po", act.at[sib_rows, :], out_cols, rx_a, whole_cut)
    stages = [act.at[pl.ds(0, rows), pl.ds(3 * half, half)], gp.at[pl.ds(0, rows), pl.ds(3 * half, half)]]
    outs = [block_out.at[:, pl.ds(h * half, half)] for h in range(2)]
    at_b = wires.at("bo", 0, 2), wires.at("bo", 1, 2)

    ok_from, ok_to = gains.at[0], gains_rx.at[0]

    def finish_block():
        tensor_end("po", dot(act[own_rows, :], wb[...]), rx_a, whole_cut)
        for h in range(2):
            cols = pl.ds(h * half, half)
            stages[h][...] = (x1[:, cols] + rx_a[:, cols]).astype(bf16)
        send("ok", ok_from, ok_to, sib)

    def send_block(h):
        return lambda: wires.send_or_keep(swapped, at_b[0] + h, at_b[1] + h, stages[h], outs[h], outs[h], diag)

    do["finish"], do["bo0"], do["bo1"] = finish_block, send_block(0), send_block(1)

    run(plan("GO"))
    recv("dx", dxb.at[sib_rows], sib)

    for j in range(2):
        go[pl.ds(j * half, half)] = dot_tn(o_all[j], dxb[:, head_rows]).astype(bf16)
    wires.sent("feat")
    run(plan("PB"))

    def project_back(i):
        at = pl.ds(pl.multiple_of(i * rows, 128), rows)
        grad = dot_nt(dxb[at, pl.ds(0, half)], wo[0, head_rows]) + dot_nt(
            dxb[at, pl.ds(half, half)], wo[1, head_rows]
        )
        live = 1.0 - feat[at][:, pad_mark : pad_mark + 1].astype(f32)
        do_all[at] = (grad.astype(bf16).astype(f32) * live * inv[at]).astype(bf16)

    loop(2, project_back)

    swap_heads = head_matrix(128, 1.0, True)

    def attend_back(p, q_at, k_at, first):
        q, k, v = head_pair(qn, q_at, p), head_pair(kn, k_at, p), head_pair(vn, k_at, p)
        grad = head_pair(do_all, q_at, p)
        lane_at = pl.ds(pl.multiple_of(p * 128, 128), 128)
        product = grad.astype(f32) * o_all[c, q_at, lane_at].astype(f32)
        delta = split_dot(product, swap_heads)
        d0 = delta.astype(bf16).astype(f32)
        d1 = (delta - d0).astype(bf16).astype(f32)
        d2 = delta - d0 - d1
        spot = lanes(delta.shape) % HD
        rider = jnp.where(spot == 0, -d0, jnp.where(spot == 1, -d1, jnp.where(spot == 2, -d2, 0.0))).astype(bf16)
        fq_, _ = masks(q_at)
        _, fk = masks(k_at)
        dqs, dks, dvs = [], [], []
        for parity in range(2):
            mine = lambda a, b: jnp.where(low_head(a.shape) == (parity == 0), a, b)
            weights = jnp.exp(dot_nt(mine(k, fk), mine(q, fq_)))
            slopes = dot_nt(mine(v, jnp.ones_like(v)), mine(grad, rider))
            dscores = (weights * slopes).astype(bf16)
            dvs.append(dot(weights.astype(bf16), grad))
            dks.append(dot(dscores, q))
            dqs.append(dot_tn(dscores, k))
        merge = lambda pair: jnp.where(low_head(pair[0].shape), pair[0], pair[1])
        dqp[q_at] = merge(dqs)
        for ref, parts in ((dkp, dks), (dvp, dvs)):
            ref[k_at] = merge(parts) if first else ref[k_at] + merge(parts)

    dproj = gp.at[:, pl.ds(0, 3 * half)]

    def head_back(p):
        lane_at = pl.ds(pl.multiple_of(p * 128, 128), 128)

        for i in range(2):
            at = pl.ds(i * rows, rows)
            for part, source, gain_row, scale_by in ((0, dqp, 2, HD**-0.5), (1, dkp, 3, 1.0)):
                lane_all = pl.ds(pl.multiple_of(c * half + p * 128, 128), 128)
                gain = gains[4, pl.ds(gain_row, 1), lane_all]
                centred = cen[at, pl.ds(pl.multiple_of(part * half + p * 128, 128), 128)].astype(f32)
                scale = lax.rsqrt(dot((centred * centred).astype(bf16), pair_mean) + 1e-6)
                normed = centred * scale
                grad = source[at] * scale_by if part == 0 else source[at]
                ggrad[0, pl.ds(gain_row, 1), lane_all] += jnp.sum(grad * normed, axis=0, keepdims=True)
                lifted = grad * gain
                back = scale * (
                    lifted - split_dot(lifted, pair_mean) - normed * split_dot(lifted * normed, pair_mean)
                )
                dproj[at, pl.ds(pl.multiple_of(p * pair_cols + part * 128, 128), 128)] = back.astype(bf16)
            dproj[at, pl.ds(pl.multiple_of(p * pair_cols + 256, 128), 128)] = dvp[at].astype(bf16)


    def weight_back(p):
        cols = pl.ds(pl.multiple_of(p * pair_cols, 128), pair_cols)
        act[pl.ds(0, width), cols] = dot_tn(a_all[...], dproj[:, cols]).astype(bf16)

    def back_pair(p):
        for b in range(blocks):
            steps_at("B", p, b)
            attend_back(p, block_at(b), long_at, b == 0)
        attend_back(p, short_at, short_at, True)
        head_back(p)
        weight_back(p)

    loop(pairs, back_pair)
    run(plan("PQ"))

    recv("ok", ok_to, sib)
    wires.sent("po0")

    def first_cols(rows_, cols):
        return dot_nt(rows_, wq[cols, :])

    tensor_sum("pq", dproj.at[sib_rows, :], first_cols, rx_a, two_cuts)
    run(plan("PQEND"))
    tensor_end("pq", dot_nt(dproj[own_rows, :], wq[...]), rx_a, two_cuts)
    run(plan("FIRST"))
    at_p = wires.at("pg", 0, rows // 128), wires.at("pg", 1, rows // 128)

    def first_back(i):
        here = pl.ds(pl.multiple_of(i * 128, 128), 128)
        grad = rx_a[here]
        normed, scale = norm_parts(xs[here].astype(f32), None)
        ggrad[0, 0:1, :] += jnp.sum(grad * normed, axis=0, keepdims=True)
        total = rx_b[here] + norm_back(grad, gain_first, normed, scale)
        xs[here] = total.astype(bf16)

    def send_patches(i):
        part, to = xs.at[pl.ds(i * 128, 128)], patch_out.at[pl.ds(i * 128, 128)]
        return lambda: wires.send_or_keep(swapped, at_p[0] + i, at_p[1] + i, part, to, to, diag)

    loop(rows // 128, first_back)
    for i in range(rows // 128):
        do[f"pg{i}"] = send_patches(i)
    run(plan("END"))
    rest, mine = ggrad[4], None
    for _ in range(3):
        term = rest.astype(bf16)
        part = dot_nt(term, spread_gain)
        mine = part if mine is None else mine + part
        rest = rest - term.astype(f32)
    fg[...] = mine
    put_g = pltpu.make_async_copy(fg, gg_out, wires.recv_sems.at[wires.at("gout", 1)])
    put_g.start()
    outputs.append(put_g)
    for h in range(2):
        wires.recv_at(at_b[1] + h, outs[h], diag)
    for i in range(rows // 128):
        wires.recv_at(at_p[1] + i, patch_out.at[pl.ds(i * 128, 128)], diag)
    for put in outputs:
        put.wait()
    wires.drain()
    assert wires.sizes[0] <= SEND_SEMAPHORES and wires.sizes[1] <= RECV_SEMAPHORES


def run_layer(patches, cotangent, segments, weights, gain_rows):
    rows, width = patches.shape
    full = segments.shape[1]
    half = width // 2
    pairs = half // 128
    wq_in, wo_in, wi_in, wb_in = weights
    shard = wq_in.shape[0]
    nq, no, ni = wq_in.shape[1] // 2, wo_in.shape[1] // 2, wi_in.shape[1] // 2
    nb = wb_in.shape[1]
    depth, deep = 2 * shard, wb_in.shape[0]
    vm = lambda shape, kind=bf16: pltpu.VMEM(shape, kind)
    wide = (nq, no, ni)
    third = nq // pairs
    scratch = (
        [vm((rows, width)), vm((full, width)), vm((full, 128))]
        + [vm((width, nq)), vm((2, width, no)), vm((width, ni)), vm((SPAN * deep, nb))]
        + [vm((5, 8, width), f32), vm((7, 8, width), f32)]
        + [vm((full, width)), vm((full, width)), vm((full, half)), vm((full, half)), vm((full, half))]
        + [vm((2, full, half)), vm((full, half), f32), vm((rows, width), f32), vm((full, width))]
        + [vm((full, ni)), vm((full, ni))]
        + [vm((rows, width), f32)] * 3
        + [vm((full, half))]
        + [vm((full, 128), f32)] * 3
        + [vm((5, 8, width), f32), vm((7, 8, width), f32)]
        + [vm((width, no)), vm((width, ni)), vm((SPAN * deep, nb))]
    )
    for lead in ((NZ, 2), (NZ,), (NZ - 1,)):
        scratch += [vm((pairs, *lead, depth, third)), vm((*lead, depth, no)), vm((*lead, depth, ni)), vm((*lead, deep, nb))]
    scratch += [vm((pairs, 2, shard, third), f32), vm((2, shard, no), f32), vm((2, shard, ni), f32)] * 2
    scratch += [vm((deep, nb), f32), vm((8, shard), f32)]
    scratch += [pltpu.SemaphoreType.DMA((SEND_SEMAPHORES,)), pltpu.SemaphoreType.DMA((RECV_SEMAPHORES,))]
    here = pl.BlockSpec(memory_space=pltpu.VMEM)
    away = pl.BlockSpec(memory_space=pl.ANY)
    out = lambda shape, kind=f32: jax.ShapeDtypeStruct(shape, kind)
    return pl.pallas_call(
        layer_kernel,
        out_shape=(
            out((rows, width), bf16),
            out((rows, width), bf16),
            out((pairs, 2, shard, third)),
            out((2, shard, no)),
            out((2, shard, ni)),
            out((deep, nb)),
            out((8, shard)),
        ),
        in_specs=[away, away] + [here] * 6,
        out_specs=(away,) * 7,
        scratch_shapes=scratch,
        compiler_params=pltpu.CompilerParams(
            collective_id=0, has_side_effects=True, vmem_limit_bytes=VMEM_BYTES
        ),
        name="layer",
    )(patches, cotangent, segments, wq_in, wo_in, wi_in, wb_in, gain_rows)


def adam_step(weight, grad, first, second, rate, shrink):
    first_new = beta_one * first + (1.0 - beta_one) * grad
    second_new = beta_two * second + (1.0 - beta_two) * grad * grad
    first_fix = first_new / (1.0 - beta_one**STEP)
    second_fix = second_new / (1.0 - beta_two**STEP)
    weight_new = weight - rate * (first_fix / (jnp.sqrt(second_fix) + epsilon) + shrink * weight)
    return (first_new, second_new, weight_new)


def update_kernel(*refs):
    inputs, outs, held, news = refs[:22], refs[22:39], refs[39:59], refs[59:74]
    passing, (load_sems, store_sems, pass_sems) = refs[74:76], refs[76:]
    takes = [pltpu.make_async_copy(inputs[i], passing[i], pass_sems.at[i]) for i in range(2)]
    passes = [pltpu.make_async_copy(passing[i], outs[i], pass_sems.at[2 + i]) for i in range(2)]
    loads = [pltpu.make_async_copy(inputs[2 + i], held[i], load_sems.at[i]) for i in range(20)]
    stores = [pltpu.make_async_copy(news[i], outs[2 + i], store_sems.at[i]) for i in range(15)]
    order = (3, 2, 0, 1, 4)
    for at in order:
        for i in (at, 5 + at, 10 + at, 15 + at):
            loads[i].start()
    for copy in takes:
        copy.start()
    gq, go, gi, gb, gg = held[:5]
    state = held[5:]

    def update(at, cols, grad):
        weight, first, second = state[at], state[5 + at], state[10 + at]
        values = adam_step(weight[:, cols], grad, first[:, cols], second[:, cols], rate_list[at], shrink_list[at])
        for to, value in zip(news[3 * at : 3 * at + 3], values):
            to[:, cols] = value

    width = gb.shape[1]
    half = width // 2
    for at in order:
        for i in (at, 5 + at, 10 + at, 15 + at):
            loads[i].wait()
        if at == 0:
            for h in range(2):
                for part in range(3):
                    for p in range(half // 128):
                        grad = gq[p, h, :, pl.ds(part * 128, 128)]
                        update(0, pl.ds(part * width + h * half + p * 128, 128), grad)
        elif at == 1:
            for h in range(2):
                update(1, pl.ds(h * half, half), go[h])
        elif at == 2:
            group = gi.shape[2] // 8
            for pair in range(4):
                cols = pl.ds(2 * pair * group, 2 * group)
                first, second = gi[0, :, cols], gi[1, :, cols]
                low = lanes(first.shape) < group
                update(2, pl.ds(4 * pair * group, 2 * group), jnp.where(low, first, pltpu.roll(second, group, 1)))
                cols = pl.ds((4 * pair + 2) * group, 2 * group)
                update(2, cols, jnp.where(low, pltpu.roll(first, group, 1), second))
        elif at == 3:
            update(3, slice(None), gb[...])
        else:
            update(4, slice(None), gg[0:4, :])
        for i in range(3):
            stores[3 * at + i].start()
        if at == 3:
            for take, copy in zip(takes, passes):
                take.wait()
                copy.start()
    for copy in passes + stores:
        copy.wait()


def update_all(block, patch, grads, state):
    away = pl.BlockSpec(memory_space=pl.ANY)
    like = lambda v: jax.ShapeDtypeStruct(v.shape, v.dtype)
    news = tuple(like(state[i]) for i in range(5) for _ in range(3))
    operands = (*grads, *state)
    return pl.pallas_call(
        update_kernel,
        out_shape=(like(block), like(patch)) + news,
        in_specs=[away] * 22,
        out_specs=(away,) * 17,
        scratch_shapes=[pltpu.VMEM(v.shape, v.dtype) for v in operands]
        + [pltpu.VMEM(v.shape, v.dtype) for v in news]
        + [pltpu.VMEM(v.shape, v.dtype) for v in (block, patch)]
        + [pltpu.SemaphoreType.DMA((n,)) for n in (20, 15, 4)],
        compiler_params=pltpu.CompilerParams(vmem_limit_bytes=VMEM_BYTES),
        name="update",
    )(block, patch, *operands)


def shards(spans, patches, segments, cotangent, *state):
    dp, blk = lax.axis_index("dp"), lax.axis_index("blk")
    index = dp * 2 + blk
    members = 2 * SPAN
    place = index % members
    state = [v.T if i % 5 == 4 else v for i, v in enumerate(state)]
    weights = state[:5]

    def span_rows(weight, axis=0):
        if spans == 1:
            return weight
        whole = lax.all_gather(weight, ("dp", "blk"), axis=axis, tiled=True)
        depth = whole.shape[axis] // members
        return lax.dynamic_slice_in_dim(whole, place * depth, depth, axis)

    def span_sum(grad, rows, axis=0):
        shape = [n * members if i == axis else n for i, n in enumerate(grad.shape)]
        whole = lax.dynamic_update_slice_in_dim(jnp.zeros(shape, f32), grad, place * grad.shape[axis], axis)
        whole = lax.psum(whole, ("dp", "blk"))
        return lax.dynamic_slice_in_dim(whole, index * rows, rows, axis)

    block_out, patch_grad, *grads = run_layer(
        patches[0],
        cotangent[0],
        segments,
        [span_rows(w) for w in weights[:4]],
        span_rows(weights[4], 1),
    )
    if spans > 1:
        rows = [w.shape[0] for w in weights[:4]] + [weights[4].shape[1]]
        grads = [span_sum(g, n, axis) for g, n, axis in zip(grads, rows, (2, 1, 1, 0, 1))]
    block_out, patch_grad, *news = update_all(block_out, patch_grad, grads, state)
    news = [v.T if i >= 12 else v for i, v in enumerate(news)]
    return (block_out[None], patch_grad[None], *news)


def solution(mesh):
    rows, tokens = P(("dp", "blk"), None), P("dp", "blk", None)
    return jax.shard_map(
        functools.partial(shards, mesh.shape["dp"] // SPAN),
        mesh=mesh,
        in_specs=(tokens, P("dp", None), tokens) + (rows,) * 15,
        out_specs=(tokens, tokens) + (rows,) * 15,
        check_vma=False,
    )
```

```python
import functools

import jax
import jax.numpy as jnp
from jax import lax
from jax.experimental import pallas as pl
from jax.experimental.pallas import tpu as pltpu
from jax.sharding import PartitionSpec as P

H = 12
HD = 64
STEP = 5
SPAN = 16
NZ = 4

pad_mark = 7
beta_one = 0.5
beta_two = 0.5
epsilon = 1e-08
rate_list = (0.03, 0.1, 0.03, 0.02, 0.1)
shrink_list = (0.1, 0.1, 0.1, 0.1, 0.0)

MESH = pl.DeviceIdType.MESH
f32 = jnp.float32
bf16 = jnp.bfloat16
LONG = 1024
KB = 512
PLAN = {
    "LN1": (115, 121, 116, 99, 117, 118, 122, 0, 125, 1, 100, 101, 16, 120, 119, 49, 84, 102, 17, 32, 22, 4, 103, 127, 7, 5, 48, 65, 20, 37, 104, 6, 105, 64, 9, 38, 54, 55, 106,),
    "F0": (33, 52, 36, 10, 21, 8, 24, 26, 83, 128, 56, 71, 53, 123, 25, 2, 23, 58,),
    "F1": (39, 41,),
    "F2": (57, 18, 42, 40, 68, 69,),
    "F3": (87, 50, 34,),
    "F4": (124, 70,),
    "F5": (89,),
    "OSEND": (72,),
    "OUT": (73, 74, 126,),
    "PREH": (91,),
    "H0": (90, 93, 88, 66,),
    "H1": (92,),
    "DZ": (86, 85,),
    "PIEND": (67,),
    "SECOND": (96,),
    "PO": (94, 95, 97,),
    "B1": (51, 140,),
    "B2": (3, 76,),
    "B3": (142, 141, 62, 59, 61, 60,),
    "B4": (19, 14, 11, 75, 13, 77, 12, 78, 80,),
    "PQ": (35, 63, 15, 27,),
    "PQEND": (79, 28, 133, 29, 30, 98, 131,),
    "END": (107, 144, 147, 143, 145, 146, 81, 82, 46, 134, 108, 45, 109, 132, 129, 110, 31, 43, 111, 139, 44, 112, 47, 113, 135, 137, 114, 136, 138, 130,),
}
VMEM_BYTES = 66 * 2**20 - 2**19
SEND_SEMAPHORES, RECV_SEMAPHORES = 64, 152


def dot(a, b):
    return lax.dot_general(a, b, (((1,), (0,)), ((), ())), preferred_element_type=f32)


def dot_nt(a, b):
    return lax.dot_general(a, b, (((1,), (1,)), ((), ())), preferred_element_type=f32)


def dot_tn(a, b):
    return lax.dot_general(a, b, (((0,), (0,)), ((), ())), preferred_element_type=f32)


def split_dot(value, matrix):
    high = value.astype(bf16)
    rest = (value - high.astype(f32)).astype(bf16)
    return dot(high, matrix) + dot(rest, matrix)


def lanes(shape):
    return lax.broadcasted_iota(jnp.int32, shape, len(shape) - 1)


def head_matrix(width, scale, swap):
    row = lax.broadcasted_iota(jnp.int32, (width, width), 0) // HD
    col = lax.broadcasted_iota(jnp.int32, (width, width), 1) // HD
    if swap:
        col = col + 1 - 2 * (col % 2)
    return jnp.where(row == col, scale, 0.0).astype(bf16)


def loop(count, body, before=()):
    def one(i, carry):
        for at, steps in enumerate(before):
            if steps:
                pl.when(i == at)(functools.partial(run, steps))
        body(i)
        return carry

    lax.fori_loop(0, count, one, 0)


def run(steps):
    for step in steps:
        step()


class Wires:
    def __init__(self, send_sems, recv_sems):
        self.send_sems, self.recv_sems = send_sems, recv_sems
        self.names = {}
        self.sizes = [0, 0]
        self.pending = {}

    def at(self, name, side, count=1):
        if (name, side) not in self.names:
            self.names[name, side] = self.sizes[side]
            self.sizes[side] += count
        return self.names[name, side]

    def make(self, send_at, recv_at, src, dst, dev):
        return pltpu.make_async_remote_copy(
            src_ref=src,
            dst_ref=dst,
            send_sem=self.send_sems.at[send_at],
            recv_sem=self.recv_sems.at[recv_at],
            device_id=dev,
            device_id_type=MESH,
        )

    def send(self, name, src, dst, dev):
        self.send_at(self.at(name, 0), self.at(name, 1), src, dst, dev)

    def send_at(self, send_at, recv_at, src, dst, dev):
        self.make(send_at, recv_at, src, dst, dev).start()
        self.pending[send_at] = lambda: self.make(send_at, 0, src, src, dev).wait_send()

    def send_group(self, group, whole, name, src, dst, dev):
        send_at = self.at(group, 0)
        self.make(send_at, self.at(name, 1), src, dst, dev).start()
        self.pending[send_at] = lambda: self.make(send_at, 0, whole, whole, dev).wait_send()

    def recv(self, name, dst, dev):
        self.recv_at(self.at(name, 1), dst, dev)

    def recv_at(self, at, dst, dev):
        self.make(0, at, dst, dst, dev).wait_recv()

    def send_or_keep(self, remote, send_at, recv_at, src, dst, kept, dev):
        def far():
            self.make(send_at, recv_at, src, dst, dev).start()

        def near():
            pltpu.make_async_copy(src, kept, self.recv_sems.at[recv_at]).start()

        pl.when(remote)(far)
        pl.when(jnp.logical_not(remote))(near)

        def finish():
            pl.when(remote)(lambda: self.make(send_at, 0, src, dst, dev).wait_send())

        self.pending[send_at] = finish

    def sent(self, name, count=1):
        for i in range(count):
            self.pending.pop(self.at(name, 0) + i)()

    def drain(self):
        for finish in self.pending.values():
            finish()
        self.pending = {}


def layer_kernel(
    patch_in, cot_in, seg_in, wq_in, wo_in, wi_in, wb_in, gain_in,
    block_out, patch_out, gq_out, go_out, gi_out, gb_out, gg_out,
    xs, ys, feat, wq, wo, wi, wb, gains, gains_rx,
    a_all, cen, qn, kn, vn, o_all, inv, x1, b_all, act, gp, tx, rx_a, rx_b,
    do_all, dqp, dkp, dvp, ggrad, ggrad_rx,
    go, gi, gb, r1q, r1o, r1i, r1b, r2q, r2o, r2i, r2b, r3q, r3o, r3i, r3b,
    fq, fo, fi, uq, uo, ui, fb, fg,
    send_sems, recv_sems,
):
    rows, width = xs.shape
    full = a_all.shape[0]
    half = width // 2
    ff = wi.shape[1]
    pairs = half // 128
    dp, y = lax.axis_index("dp"), lax.axis_index("blk")
    base = dp // SPAN * SPAN
    z, x, c = dp % SPAN // 4, dp % 4 // 2, dp % 2
    ny, nx, nc = 1 - y, 1 - x, 1 - c
    swapped = c != y

    def dev(z_, x_, c_, y_):
        return (base + (z_ * 2 + x_) * 2 + c_, y_)

    sib = dev(z, x, nc, y)
    ynb = dev(z, x, c, ny)
    xnb = dev(z, nx, c, y)
    diag = dev(z, x, nc, ny)
    zs = [dev((z + d) % NZ, x, c, y) for d in range(NZ)]
    wires = Wires(send_sems, recv_sems)
    send, recv = wires.send, wires.recv

    barrier = pltpu.get_barrier_semaphore()
    partners = [sib, ynb, xnb, diag] + zs[1:]
    for partner in partners:
        pl.semaphore_signal(barrier, inc=1, device_id=partner, device_id_type=MESH)

    own_rows = pl.ds(pl.multiple_of(c * rows, 128), rows)
    sib_rows = pl.ds(pl.multiple_of(nc * rows, 128), rows)
    head_rows = pl.ds(pl.multiple_of(c * half, 128), half)

    def block(z_, x_, y_):
        return (z_ * 2 + x_) * 2 + y_

    def turns(o):
        no = 1 - o
        return x + o - 2 * x * o, y + no - 2 * y * no, x + no - 2 * x * no, y + o - 2 * y * o

    class Matrix:
        def __init__(self, name, weight, grad, buffers, order, early, back_order, back_early):
            first, second, third = buffers
            self.name = name
            self.early, self.back_early = early, back_early
            self.rx2_three = second.at[pl.ds(0, 3)]
            self.rx1 = [[first.at[d, r] for r in range(2)] for d in range(NZ)]
            self.rx1_both = [first.at[d] for d in range(NZ)]
            self.rx2 = [second.at[d] for d in range(NZ)]
            self.rx3 = [third.at[d] for d in range(NZ - 1)]
            self.rx3_all = third
            self.depth = weight.shape[0] // SPAN
            self.sent_weight = weight.at[pl.ds(0, 15 * self.depth)]
            self.sent_grad = grad.at[pl.ds(0, 15 * self.depth)]
            self.last_weight = weight.at[pl.ds(0, 8 * self.depth)]
            xf, yf, xs_, ys_ = turns(order)
            self.near, self.next = dev(z, xf, c, yf), dev(z, xs_, c, ys_)
            back = [(z + NZ - d) % NZ for d in range(NZ)]
            ahead = [(z + d) % NZ for d in range(NZ)]
            self.at_z = [self.at(weight, block(zd, x, y)) for zd in back]
            self.at_near = [self.at(weight, block(zd, xf, yf)) for zd in back]
            xf, yf, xs_, ys_ = turns(back_order)
            self.back_near, self.back_next = dev(z, xf, c, yf), dev(z, xs_, c, ys_)
            self.to_next = [[self.at(grad, block(zd, xs_, ys_)), self.at(grad, block(zd, nx, ny))] for zd in ahead]
            self.to_near = [self.at(grad, block(zd, xf, yf)) for zd in ahead]
            self.to_z = [self.at(grad, block(zd, x, y)) for zd in ahead]

        def at(self, ref, b):
            return ref.at[pl.ds(pl.multiple_of(b * self.depth, 16), self.depth)]

        def pass_on(self, name, piece, to):
            wires.send_group(f"{self.name}g", self.sent_weight, f"{self.name}{name}", piece, piece, to)

        def gather_own_z(self):
            for d in range(1, NZ):
                self.pass_on(f"z{d}", self.at_z[0], zs[d])

        def gather_own_near(self):
            self.pass_on("f0", self.at_z[0], self.near)
            self.pass_on("s", self.at_z[0], self.next)

        def gather_own(self):
            self.gather_own_z()
            self.gather_own_near()

        def gather_z(self, d):
            recv(f"{self.name}z{d}", self.at_z[d], zs[1])
            if not self.early:
                self.pass_on(f"f{d}", self.at_z[d], self.near)
            self.pass_on("s", self.at_z[d], self.next)

        def gather_near(self, d):
            recv(f"{self.name}f{d}", self.at_near[d], self.near)
            if self.early and d == 0:
                for k in range(1, NZ):
                    self.pass_on(f"f{k}", self.at_near[0], zs[k])
            self.pass_on("s", self.at_near[d], self.next)

        def gather_end(self):
            recv(f"{self.name}s", self.last_weight, self.next)

        def gather_steps(self):
            from_z = [functools.partial(self.gather_z, d) for d in (1, 2, 3)]
            from_near = [functools.partial(self.gather_near, d) for d in (0, 1, 2, 3)]
            return from_near[:1] + from_z + from_near[1:] if self.early else from_z + from_near

        def back(self, name, piece, landed, to):
            wires.send_group(f"{self.name}r", self.sent_grad, f"{self.name}{name}", piece, landed, to)

        def reduce_start(self):
            for d in (1, 2, 3, 0):
                for r in (1, 0):
                    self.back(f"a{d}", self.to_next[d][r], self.rx1[d][r], self.back_next)

        def add(self, piece, landed):
            def some(i):
                at = pl.ds(pl.multiple_of(i * 16, 16), 16)
                piece[at] = (piece[at].astype(f32) + landed[at].astype(f32)).astype(bf16)

            loop(self.depth // 16, some)

        def reduce_next(self, d):
            recv(f"{self.name}a{d}", self.rx1_both[d], self.back_next)
            self.add(self.to_near[d], self.rx1[d][1])
            if not self.back_early:
                self.back(f"b{d}", self.to_near[d], self.rx2[d], self.back_near)
            elif d:
                self.back("e", self.to_near[d], self.rx2[d - 1], zs[d])
            self.add(self.to_z[d], self.rx1[d][0])
            if self.back_early and d:
                self.back("c", self.to_z[d], self.rx3[d - 1], zs[d])

        def reduce_near(self, d):
            recv(f"{self.name}b{d}", self.rx2[d], self.back_near)
            self.add(self.to_z[d], self.rx2[d])
            if d:
                self.back("c", self.to_z[d], self.rx3[d - 1], zs[d])

        def reduce_near_early(self):
            recv(f"{self.name}e", self.rx2_three, zs[1])
            total = self.to_near[0][...].astype(f32)
            for landed in self.rx2[:3]:
                total = total + landed[...].astype(f32)
            self.to_near[0][...] = total.astype(bf16)
            self.back("n", self.to_near[0], self.rx2[3], self.back_near)

        def reduce_end(self):
            recv(f"{self.name}c", self.rx3_all, zs[1])
            total = self.to_z[0][...].astype(f32)
            for landed in self.rx3:
                total = total + landed[...].astype(f32)
            if self.back_early:
                recv(f"{self.name}n", self.rx2[3], self.back_near)
                total = total + self.rx2[3][...].astype(f32)
            return total

        def reduce_steps(self):
            first = [functools.partial(self.reduce_next, d) for d in (1, 2, 3, 0)]
            if self.back_early:
                return first, [self.reduce_near_early]
            return first, [functools.partial(self.reduce_near, d) for d in (1, 2, 3, 0)]

    pair_cols = 3 * 128
    gq = [act.at[pl.ds(0, width), pl.ds(p * pair_cols, pair_cols)] for p in range(pairs)]
    mq = [
        Matrix(
            f"q{p}", wq.at[:, pl.ds(p * pair_cols, pair_cols)], gq[p], (r1q.at[p], r2q.at[p], r3q.at[p]), 0, False, c, True
        )
        for p in range(pairs)
    ]
    mo = Matrix("o", wo.at[c], go, (r1o, r2o, r3o), 0, False, 0, True)
    mi = Matrix("i", wi, gi, (r1i, r2i, r3i), c, True, c, False)
    mb = Matrix("b", wb, gb, (r1b, r2b, r3b), c, False, c, True)

    padded = -(-wq_in.shape[0] // 16) * 16

    def pieces(at, cols):
        return lambda h: gi.at[pl.ds(pl.multiple_of((2 * at + h) * padded, 16), padded), pl.ds(0, cols)]

    sq, rq = pieces(0, wq.shape[1]), pieces(1, wq.shape[1])
    so, ro = pieces(2, half), pieces(3, half)
    si, ri = pieces(4, ff), pieces(5, ff)

    def spread(name, staged, landed):
        to, at = wires.at(f"{name}first", 1, 2) + y, wires.at(f"{name}first", 0, 2)
        other, same, slot = staged(nc), staged(c), landed(y)
        far, near = dev(z, x, nc, c), dev(z, x, c, c)

        def go_on():
            wires.send_at(at, to, other, slot, far)
            wires.send_or_keep(swapped, at + 1, to, same, slot, slot, near)

        return go_on

    def collect(name, landed, *fills):
        at = wires.at(f"{name}first", 1, 2)
        slots = [landed(p) for p in range(2)]

        def go_on():
            for p in range(2):
                wires.recv_at(at + p, slots[p], sib)
            for matrix, cols in fills:
                fill(slots, matrix, cols)

        return go_on

    def fill(slots, matrix, cols):
        parts = [slot[:, cols].astype(f32)[: matrix.depth // 2] for slot in slots]
        matrix.at_z[0][...] = jnp.concatenate(parts, 0).astype(bf16)

    def unspread(name, matrix, ready, landed):
        to, at = wires.at(f"{name}last", 1, 2), wires.at(f"{name}last", 0, 2)
        far, near = dev(z, x, y, ny), dev(z, x, y, y)
        depth = matrix.depth // 2
        slot_at = to + c
        other, same, slot = ready.at[ny], ready.at[y], landed.at[c]

        def go_on():
            total = matrix.reduce_end()
            for p in range(2):
                ready[p] = total[p * depth : (p + 1) * depth]
            wires.send_at(at, slot_at, other, slot, far)
            wires.send_or_keep(swapped, at + 1, slot_at, same, slot, slot, near)

        return go_on

    def unspread_end(name, landed, out):
        at = wires.at(f"{name}last", 1, 2)
        slots = [landed.at[p] for p in range(2)]
        put = pltpu.make_async_copy(landed, out, wires.recv_sems.at[wires.at(f"{name}out", 1)])
        outputs.append(put)

        def go_on():
            for p in range(2):
                wires.recv_at(at + p, slots[p], sib)
            put.start()

        return go_on

    outputs = []

    def sum_hops(name, own, landed, order):
        own, landed = [own.at[k] for k in range(5)], [landed.at[k] for k in range(7)]

        def one(k, partner):
            def start():
                send(f"{name}{k}", own[k], landed[k], partner)

            def end():
                recv(f"{name}{k}", landed[k], partner)
                own[k + 1][...] = own[k][...] + landed[k][...]

            return start, end

        def along_z(k):
            def start():
                for d in range(1, NZ):
                    send(f"{name}z{d}", own[k], landed[3 + d], zs[d])

            def end():
                total = own[k][...]
                for d in range(1, NZ):
                    recv(f"{name}z{d}", landed[3 + d], zs[1])
                    total = total + landed[3 + d][...]
                own[k + 1][...] = total

            return start, end

        return [along_z(k) if who is None else one(k, who) for k, who in enumerate(order)]

    def place_lanes(depth):
        row = lax.broadcasted_iota(jnp.int32, (depth, width), 0)
        spot = ((z * 2 + x) * 2 + c) * 2 + y
        return lanes((depth, width)) == row + spot * depth

    feat_own, feat_rx = do_all.at[:, pl.ds(0, 128)], do_all.at[:, pl.ds(128, 128)]
    gains[0] = jnp.zeros_like(gains[0])
    spread_gain = jnp.where(place_lanes(gain_in.shape[1]), 1.0, 0.0).astype(bf16)
    gains[0, 0:4, :] = dot(gain_in[...].astype(bf16), spread_gain)
    seg_lane = lax.broadcasted_iota(jnp.int32, (128, full), 0) % HD
    feat_own[...] = jnp.where(seg_lane == seg_in[...], 1.0, 0.0).astype(bf16).T
    depth = wq_in.shape[0]
    pad = jnp.zeros((padded - depth, 128), f32)
    for h in range(2):
        for p in range(pairs):
            for part in range(3):
                take = wq_in[:, pl.ds(part * width + h * half + p * 128, 128)]
                sq(h)[:, pl.ds(p * pair_cols + part * 128, 128)] = jnp.concatenate([take, pad], 0).astype(bf16)
    def prepare():
        pad = jnp.zeros((padded - depth, half), f32)
        for h in range(2):
            so(h)[...] = jnp.concatenate([wo_in[:, pl.ds(h * half, half)], pad], 0).astype(bf16)
        group = ff // 8
        pad = jnp.zeros((padded - depth, 2 * group), f32)
        for pair in range(4):
            even = wi_in[:, pl.ds(4 * pair * group, 2 * group)]
            odd = wi_in[:, pl.ds((4 * pair + 2) * group, 2 * group)]
            low_lane = lanes(even.shape) < group
            first = jnp.where(low_lane, even, pltpu.roll(odd, group, 1))
            second = jnp.where(low_lane, pltpu.roll(even, group, 1), odd)
            for h, value in enumerate((first, second)):
                si(h)[:, pl.ds(2 * pair * group, 2 * group)] = jnp.concatenate([value, pad], 0).astype(bf16)
        mb.at_z[0][...] = wb_in[...].astype(bf16)

    do = {}

    def plan(slot):
        steps = list(do.values())
        return [steps[k] for k in PLAN.get(slot, ())]

    def plans(slot, count):
        return [plan(f"{slot}{t}") for t in range(count)]

    for matrix in (*mq, mo, mi, mb):
        name = matrix.name
        do[f"{name}z"], do[f"{name}n"] = matrix.gather_own_z, matrix.gather_own_near
        do[f"{name}.end"], do[f"{name}.rs"] = matrix.gather_end, matrix.reduce_start
        first_steps, rest_steps = matrix.reduce_steps()
        for kind, steps in (("g", matrix.gather_steps()), ("a", first_steps), ("r", rest_steps)):
            for k, step in enumerate(steps):
                do[f"{name}.{kind}{k}"] = step
    for prefix, hops, keys in (
        ("", sum_hops("gain", gains, gains_rx, (ynb, None, xnb, sib)), "yzxs"),
        ("t", sum_hops("gg", ggrad, ggrad_rx, (ynb, sib, xnb, None)), "ysxz"),
    ):
        for key, (start, end) in zip(keys, hops):
            do[f"{prefix}h{key}0"], do[f"{prefix}h{key}1"] = start, end
    all_cols = slice(None)
    do["sq"], do["so"], do["si"] = spread("q", sq, rq), spread("o", so, ro), spread("i", si, ri)
    do["cq"] = collect("q", rq, *[(mq[p], pl.ds(p * pair_cols, pair_cols)) for p in range(pairs)])
    do["co"], do["ci"] = collect("o", ro, (mo, all_cols)), collect("i", ri, (mi, all_cols))
    do["prep"] = prepare
    xs_at, ys_at = (wires.at("xs", 0), wires.at("xs", 1)), (wires.at("ys", 0), wires.at("ys", 1))
    ys_own, ys_sib, wo_mine, wo_other = ys.at[own_rows], ys.at[sib_rows], wo.at[c], wo.at[nc]
    do["xs"] = lambda: wires.send_or_keep(swapped, *xs_at, patch_in, xs, xs, diag)
    do["ys"] = lambda: wires.send_or_keep(swapped, *ys_at, cot_in, ys_sib, ys_own, diag)
    do["share"] = lambda: send("wo", wo_mine, wo_mine, sib)
    do["feat"] = lambda: send("feat", feat_own, feat_rx, sib)

    def pass_cotangent():
        wires.recv_at(ys_at[1], ys_own, diag)
        send("yy", ys_own, ys_own, sib)

    def pick_feat():
        recv("feat", feat_rx, sib)
        feat[...] = jnp.where(swapped, feat_rx[...], feat_own[...])

    a_sib = a_all.at[sib_rows]
    do["ysr"], do["featr"] = pass_cotangent, pick_feat
    do["ar"] = lambda: recv("a", a_sib, sib)
    ends = [("i", mi, fi, ui, gi_out), ("o", mo, fo, uo, go_out)]
    ends += [(f"q{p}", mq[p], fq.at[p], uq.at[p], gq_out.at[p]) for p in range(pairs)]
    for name, matrix, ready, landed, out in ends:
        do[f"{name}.e"] = unspread(name, matrix, ready, landed)
        do[f"{name}.p"] = unspread_end(name, landed, out)
    put_b = pltpu.make_async_copy(fb, gb_out, wires.recv_sems.at[wires.at("bout", 1)])
    outputs.append(put_b)

    def end_b():
        fb[...] = mb.reduce_end()
        put_b.start()

    do["b.e"] = end_b

    pl.semaphore_wait(barrier, len(partners))
    run(plan("LN1"))
    gain_first, gain_second = gains[4, 0:1, :], gains[4, 1:2, :]
    wires.recv_at(xs_at[1], xs, diag)

    def norm_one(i):
        v = xs[pl.ds(pl.multiple_of(i * 128, 128), 128)].astype(f32)
        centred = v - jnp.mean(v, axis=-1, keepdims=True)
        spread_ = jnp.mean(centred * centred, axis=-1, keepdims=True)
        normed = centred * lax.rsqrt(spread_ + 1e-6) * gain_first
        a_all[pl.ds(pl.multiple_of(c * rows + i * 128, 128), 128)] = normed.astype(bf16)

    loop(rows // 128, norm_one)
    send("a", a_all.at[own_rows], a_all.at[own_rows], sib)
    pair_mean = head_matrix(128, 1.0 / HD, False)

    def project(p):
        lane_at = pl.ds(pl.multiple_of(p * 128, 128), 128)
        lane_all = pl.ds(pl.multiple_of(c * half + p * 128, 128), 128)

        def some(i):
            at = pl.ds(pl.multiple_of(i * rows, 128), rows)
            projected = dot(a_all[at], wq[:, pl.ds(pl.multiple_of(p * pair_cols, 128), pair_cols)])
            for part, to in ((0, qn), (1, kn)):
                value = projected[:, part * 128 : (part + 1) * 128]
                centred = value - split_dot(value, pair_mean)
                spread_ = dot((centred * centred).astype(bf16), pair_mean)
                cen[at, pl.ds(pl.multiple_of(part * half + p * 128, 128), 128)] = centred.astype(bf16)
                normed = (centred * lax.rsqrt(spread_ + 1e-6) * gains[4, pl.ds(2 + part, 1), lane_all]).astype(bf16)
                to[at, lane_at] = normed * (HD**-0.5) if part == 0 else normed
            vn[at, lane_at] = projected[:, 256:].astype(bf16)

        loop(2, some)

    low_head = lambda shape: lanes(shape) < HD

    def head_pair(ref, at, p):
        return ref[at, pl.ds(pl.multiple_of(p * 128, 128), 128)]

    def masks(at):
        one_hot = feat[at]
        return one_hot, (one_hot.astype(f32) * 128.0 - 128.0).astype(bf16)

    def attend(p, q_at, k_at):
        q, k, v = head_pair(qn, q_at, p), head_pair(kn, k_at, p), head_pair(vn, k_at, p)
        fq_, _ = masks(q_at)
        _, fk = masks(k_at)
        out = []
        for parity in range(2):
            mine = lambda a, b: jnp.where(low_head(a.shape) == (parity == 0), a, b)
            scores = dot_nt(mine(q, fq_), mine(k, fk))
            weights = jnp.exp(scores).astype(bf16)
            out.append(dot(weights, mine(v, jnp.ones_like(v))))
        return out

    def finish_attend(p, at, r0, r1):
        low = low_head(r0.shape)
        inverse = 1.0 / pltpu.roll(jnp.where(low, r1, r0), HD, 1)
        live = 1.0 - feat[at][:, pad_mark : pad_mark + 1].astype(f32)
        lane_at = pl.ds(pl.multiple_of(p * 128, 128), 128)
        inv[at, lane_at] = inverse
        o_all[c, at, lane_at] = (jnp.where(low, r0, r1) * inverse * live).astype(bf16)

    long_at, short_at = pl.ds(0, LONG), pl.ds(LONG, full - LONG)
    blocks = LONG // KB

    def block_at(b):
        return pl.ds(b * KB, KB)

    def steps_at(slot, p, b):
        for at in range(pairs):
            steps = plan(f"{slot}{at * blocks + b}")
            if steps:
                pl.when(p == at)(functools.partial(run, steps))

    def attend_step(t):
        p, b = t // blocks, t % blocks
        pl.when(b == 0)(lambda: project(p))
        parts = attend(p, long_at, pl.ds(pl.multiple_of(b * KB, KB), KB))

        @pl.when(b == 0)
        def _():
            for ref, part in zip((dkp, dvp), parts):
                ref[long_at] = part

        @pl.when(b > 0)
        def _():
            for ref, part in zip((dkp, dvp), parts):
                ref[long_at] += part

        @pl.when(b == blocks - 1)
        def _():
            finish_attend(p, long_at, dkp[long_at], dvp[long_at])
            finish_attend(p, short_at, *attend(p, short_at, short_at))

    loop(pairs * blocks, attend_step, plans("F", pairs * blocks))
    run(plan("OSEND"))
    send("o", o_all.at[c], o_all.at[c], sib)
    run(plan("OUT"))
    recv("wo", wo_other, sib)
    recv("o", o_all.at[nc], sib)

    def norm_parts(value, gain):
        centred = value - jnp.mean(value, axis=-1, keepdims=True)
        spread_ = jnp.mean(centred * centred, axis=-1, keepdims=True)
        scale = lax.rsqrt(spread_ + 1e-6)
        return centred * scale, scale

    step_rows = rows // 2

    def project_out(i):
        here = pl.ds(pl.multiple_of(i * step_rows, 64), step_rows)
        there = pl.ds(pl.multiple_of(c * rows + i * step_rows, 64), step_rows)
        o0, o1 = o_all[0, there], o_all[1, there]
        for j in range(2):
            cols = pl.ds(j * half, half)
            mixed = dot(o0, wo[j, pl.ds(0, half)]) + dot(o1, wo[j, pl.ds(half, half)])
            x1[here, cols] = xs[here, cols].astype(f32) + mixed
        normed, _ = norm_parts(x1[here], None)
        b_all[there] = (normed * gain_second).astype(bf16)

    for i in range(2):
        project_out(i)
        part = b_all.at[pl.ds(pl.multiple_of(c * rows + i * step_rows, 64), step_rows)]
        send(f"b{i}", part, part, sib)
    run(plan("PREH"))
    recv("yy", ys_sib, sib)
    for i in range(2):
        recv(f"b{i}", b_all.at[pl.ds(pl.multiple_of(nc * rows + i * step_rows, 64), step_rows)], sib)

    root = 0.7978845608028654

    def hidden(n):
        at = pl.ds(pl.multiple_of(n * 256, 256), 256)
        zed = dot(b_all[at], wi[...])
        square = zed * zed
        gate = 0.5 + 0.5 * jnp.tanh(zed * (root + (root * 0.044715) * square))
        activated = zed * gate
        slope = gate + (activated - activated * gate) * (2.0 * root + (6.0 * root * 0.044715) * square)
        act[at] = activated.astype(bf16)
        gp[at] = slope.astype(bf16)

    loop(full // 256, hidden, [plan("H0")] + [()] * (full // 256 - 1))

    def back_grad(n):
        cols = pl.ds(pl.multiple_of(n * 512, 512), 512)
        gb[cols] = dot_tn(act[:, cols], ys[...]).astype(bf16)

    loop(ff // 512, back_grad, [plan("H1"), plan("H2"), ()])
    run(plan("DZ"))

    def hidden_back(n):
        cols = pl.ds(pl.multiple_of(n * 512, 512), 512)
        gp[:, cols] = (dot_nt(ys[...], wb[cols, :]) * gp[:, cols].astype(f32)).astype(bf16)

    loop(ff // 512, hidden_back)

    def tensor_sum(name, rows_of_sib, cols_of, landed, cuts):
        for n, cut in enumerate(zip(cuts, cuts[1:])):
            cols = pl.ds(cut[0], cut[1] - cut[0])
            tx[:, cols] = cols_of(rows_of_sib[...], cols)
            send(f"{name}{n}", tx.at[:, cols], landed.at[:, cols], sib)

    def tensor_end(name, part, landed, cuts):
        for n, cut in enumerate(zip(cuts, cuts[1:])):
            cols = pl.ds(cut[0], cut[1] - cut[0])
            recv(f"{name}{n}", landed.at[:, cols], sib)
        for r in range(0, rows, 128):
            landed[r : r + 128] = part[r : r + 128] + landed[r : r + 128]

    whole_cut, two_cuts = (0, width), (0, width - 256, width)

    def in_cols(rows_, cols):
        return dot_nt(rows_, wi[cols, :])

    def out_cols(rows_, cols):
        return dot(rows_, wb[:, cols])

    for name in ("q", "o", "i"):
        wires.sent(f"{name}first", 2)
    run(plan("PI"))
    tensor_sum("pi", gp.at[sib_rows, :], in_cols, rx_b, whole_cut)

    def hidden_grad(n):
        cols = pl.ds(pl.multiple_of(n * 512, 512), 512)
        gi[:, cols] = dot_tn(b_all[...], gp[:, cols]).astype(bf16)

    run(plan("GI"))
    loop(ff // 512, hidden_grad)
    free_from, free_to = gains.at[1], gains_rx.at[1]
    send("free", free_from, free_to, sib)
    run(plan("PIEND"))
    tensor_end("pi", dot_nt(gp[own_rows, :], wi[...]), rx_b, whole_cut)

    ggrad[0] = jnp.zeros_like(ggrad[0])
    for i in range(2):
        wires.sent(f"b{i}")
    dxb = b_all

    def norm_back(grad, gain, normed, scale):
        lifted = grad * gain
        return scale * (
            lifted
            - jnp.mean(lifted, axis=-1, keepdims=True)
            - normed * jnp.mean(lifted * normed, axis=-1, keepdims=True)
        )

    def second_back(i):
        here = pl.ds(pl.multiple_of(i * 128, 128), 128)
        there = pl.ds(pl.multiple_of(c * rows + i * 128, 128), 128)
        grad = rx_b[here]
        normed, scale = norm_parts(x1[here], None)
        ggrad[0, 1:2, :] += jnp.sum(grad * normed, axis=0, keepdims=True)
        total = ys[there].astype(f32) + norm_back(grad, gain_second, normed, scale)
        rx_b[here] = total
        dxb[there] = total.astype(bf16)

    run(plan("SECOND"))
    loop(rows // 128, second_back)
    recv("free", free_to, sib)
    send("dx", dxb.at[own_rows], dxb.at[own_rows], sib)
    wires.sent("pi0")
    run(plan("PO"))
    tensor_sum("po", act.at[sib_rows, :], out_cols, rx_a, whole_cut)
    stages = [act.at[pl.ds(0, rows), pl.ds(3 * half, half)], gp.at[pl.ds(0, rows), pl.ds(3 * half, half)]]
    outs = [block_out.at[:, pl.ds(h * half, half)] for h in range(2)]
    at_b = wires.at("bo", 0, 2), wires.at("bo", 1, 2)

    ok_from, ok_to = gains.at[0], gains_rx.at[0]

    def finish_block():
        tensor_end("po", dot(act[own_rows, :], wb[...]), rx_a, whole_cut)
        for h in range(2):
            cols = pl.ds(h * half, half)
            stages[h][...] = (x1[:, cols] + rx_a[:, cols]).astype(bf16)
        send("ok", ok_from, ok_to, sib)

    def send_block(h):
        return lambda: wires.send_or_keep(swapped, at_b[0] + h, at_b[1] + h, stages[h], outs[h], outs[h], diag)

    do["finish"], do["bo0"], do["bo1"] = finish_block, send_block(0), send_block(1)

    run(plan("GO"))
    recv("dx", dxb.at[sib_rows], sib)

    for j in range(2):
        go[pl.ds(j * half, half)] = dot_tn(o_all[j], dxb[:, head_rows]).astype(bf16)
    wires.sent("feat")
    run(plan("PB"))

    def project_back(i):
        at = pl.ds(pl.multiple_of(i * rows, 128), rows)
        grad = dot_nt(dxb[at, pl.ds(0, half)], wo[0, head_rows]) + dot_nt(
            dxb[at, pl.ds(half, half)], wo[1, head_rows]
        )
        live = 1.0 - feat[at][:, pad_mark : pad_mark + 1].astype(f32)
        do_all[at] = (grad.astype(bf16).astype(f32) * live * inv[at]).astype(bf16)

    loop(2, project_back)

    swap_heads = head_matrix(128, 1.0, True)

    def attend_back(p, q_at, k_at, first):
        q, k, v = head_pair(qn, q_at, p), head_pair(kn, k_at, p), head_pair(vn, k_at, p)
        grad = head_pair(do_all, q_at, p)
        lane_at = pl.ds(pl.multiple_of(p * 128, 128), 128)
        product = grad.astype(f32) * o_all[c, q_at, lane_at].astype(f32)
        delta = split_dot(product, swap_heads)
        d0 = delta.astype(bf16).astype(f32)
        d1 = (delta - d0).astype(bf16).astype(f32)
        d2 = delta - d0 - d1
        spot = lanes(delta.shape) % HD
        rider = jnp.where(spot == 0, -d0, jnp.where(spot == 1, -d1, jnp.where(spot == 2, -d2, 0.0))).astype(bf16)
        fq_, _ = masks(q_at)
        _, fk = masks(k_at)
        dqs, dks, dvs = [], [], []
        for parity in range(2):
            mine = lambda a, b: jnp.where(low_head(a.shape) == (parity == 0), a, b)
            weights = jnp.exp(dot_nt(mine(k, fk), mine(q, fq_)))
            slopes = dot_nt(mine(v, jnp.ones_like(v)), mine(grad, rider))
            dscores = (weights * slopes).astype(bf16)
            dvs.append(dot(weights.astype(bf16), grad))
            dks.append(dot(dscores, q))
            dqs.append(dot_tn(dscores, k))
        merge = lambda pair: jnp.where(low_head(pair[0].shape), pair[0], pair[1])
        dqp[q_at] = merge(dqs)
        for ref, parts in ((dkp, dks), (dvp, dvs)):
            ref[k_at] = merge(parts) if first else ref[k_at] + merge(parts)

    dproj = gp.at[:, pl.ds(0, 3 * half)]

    def head_back(p):
        lane_at = pl.ds(pl.multiple_of(p * 128, 128), 128)

        for i in range(2):
            at = pl.ds(i * rows, rows)
            for part, source, gain_row, scale_by in ((0, dqp, 2, HD**-0.5), (1, dkp, 3, 1.0)):
                lane_all = pl.ds(pl.multiple_of(c * half + p * 128, 128), 128)
                gain = gains[4, pl.ds(gain_row, 1), lane_all]
                centred = cen[at, pl.ds(pl.multiple_of(part * half + p * 128, 128), 128)].astype(f32)
                scale = lax.rsqrt(dot((centred * centred).astype(bf16), pair_mean) + 1e-6)
                normed = centred * scale
                grad = source[at] * scale_by if part == 0 else source[at]
                ggrad[0, pl.ds(gain_row, 1), lane_all] += jnp.sum(grad * normed, axis=0, keepdims=True)
                lifted = grad * gain
                back = scale * (
                    lifted - split_dot(lifted, pair_mean) - normed * split_dot(lifted * normed, pair_mean)
                )
                dproj[at, pl.ds(pl.multiple_of(p * pair_cols + part * 128, 128), 128)] = back.astype(bf16)
            dproj[at, pl.ds(pl.multiple_of(p * pair_cols + 256, 128), 128)] = dvp[at].astype(bf16)


    def weight_back(p):
        cols = pl.ds(pl.multiple_of(p * pair_cols, 128), pair_cols)
        act[pl.ds(0, width), cols] = dot_tn(a_all[...], dproj[:, cols]).astype(bf16)

    def back_pair(p):
        for b in range(blocks):
            steps_at("B", p, b)
            attend_back(p, block_at(b), long_at, b == 0)
        attend_back(p, short_at, short_at, True)
        head_back(p)
        weight_back(p)

    loop(pairs, back_pair)
    run(plan("PQ"))

    recv("ok", ok_to, sib)
    wires.sent("po0")

    def first_cols(rows_, cols):
        return dot_nt(rows_, wq[cols, :])

    tensor_sum("pq", dproj.at[sib_rows, :], first_cols, rx_a, two_cuts)
    run(plan("PQEND"))
    tensor_end("pq", dot_nt(dproj[own_rows, :], wq[...]), rx_a, two_cuts)
    run(plan("FIRST"))
    at_p = wires.at("pg", 0, rows // 128), wires.at("pg", 1, rows // 128)

    def first_back(i):
        here = pl.ds(pl.multiple_of(i * 128, 128), 128)
        grad = rx_a[here]
        normed, scale = norm_parts(xs[here].astype(f32), None)
        ggrad[0, 0:1, :] += jnp.sum(grad * normed, axis=0, keepdims=True)
        total = rx_b[here] + norm_back(grad, gain_first, normed, scale)
        xs[here] = total.astype(bf16)

    def send_patches(i):
        part, to = xs.at[pl.ds(i * 128, 128)], patch_out.at[pl.ds(i * 128, 128)]
        return lambda: wires.send_or_keep(swapped, at_p[0] + i, at_p[1] + i, part, to, to, diag)

    loop(rows // 128, first_back)
    for i in range(rows // 128):
        do[f"pg{i}"] = send_patches(i)
    run(plan("END"))
    rest, mine = ggrad[4], None
    for _ in range(3):
        term = rest.astype(bf16)
        part = dot_nt(term, spread_gain)
        mine = part if mine is None else mine + part
        rest = rest - term.astype(f32)
    fg[...] = mine
    put_g = pltpu.make_async_copy(fg, gg_out, wires.recv_sems.at[wires.at("gout", 1)])
    put_g.start()
    outputs.append(put_g)
    for h in range(2):
        wires.recv_at(at_b[1] + h, outs[h], diag)
    for i in range(rows // 128):
        wires.recv_at(at_p[1] + i, patch_out.at[pl.ds(i * 128, 128)], diag)
    for put in outputs:
        put.wait()
    wires.drain()
    assert wires.sizes[0] <= SEND_SEMAPHORES and wires.sizes[1] <= RECV_SEMAPHORES


def run_layer(patches, cotangent, segments, weights, gain_rows):
    rows, width = patches.shape
    full = segments.shape[1]
    half = width // 2
    pairs = half // 128
    wq_in, wo_in, wi_in, wb_in = weights
    shard = wq_in.shape[0]
    nq, no, ni = wq_in.shape[1] // 2, wo_in.shape[1] // 2, wi_in.shape[1] // 2
    nb = wb_in.shape[1]
    depth, deep = 2 * shard, wb_in.shape[0]
    vm = lambda shape, kind=bf16: pltpu.VMEM(shape, kind)
    wide = (nq, no, ni)
    third = nq // pairs
    scratch = (
        [vm((rows, width)), vm((full, width)), vm((full, 128))]
        + [vm((width, nq)), vm((2, width, no)), vm((width, ni)), vm((SPAN * deep, nb))]
        + [vm((5, 8, width), f32), vm((7, 8, width), f32)]
        + [vm((full, width)), vm((full, width)), vm((full, half)), vm((full, half)), vm((full, half))]
        + [vm((2, full, half)), vm((full, half), f32), vm((rows, width), f32), vm((full, width))]
        + [vm((full, ni)), vm((full, ni))]
        + [vm((rows, width), f32)] * 3
        + [vm((full, half))]
        + [vm((full, 128), f32)] * 3
        + [vm((5, 8, width), f32), vm((7, 8, width), f32)]
        + [vm((width, no)), vm((width, ni)), vm((SPAN * deep, nb))]
    )
    for lead in ((NZ, 2), (NZ,), (NZ - 1,)):
        scratch += [vm((pairs, *lead, depth, third)), vm((*lead, depth, no)), vm((*lead, depth, ni)), vm((*lead, deep, nb))]
    scratch += [vm((pairs, 2, shard, third), f32), vm((2, shard, no), f32), vm((2, shard, ni), f32)] * 2
    scratch += [vm((deep, nb), f32), vm((8, shard), f32)]
    scratch += [pltpu.SemaphoreType.DMA((SEND_SEMAPHORES,)), pltpu.SemaphoreType.DMA((RECV_SEMAPHORES,))]
    here = pl.BlockSpec(memory_space=pltpu.VMEM)
    away = pl.BlockSpec(memory_space=pl.ANY)
    out = lambda shape, kind=f32: jax.ShapeDtypeStruct(shape, kind)
    return pl.pallas_call(
        layer_kernel,
        out_shape=(
            out((rows, width), bf16),
            out((rows, width), bf16),
            out((pairs, 2, shard, third)),
            out((2, shard, no)),
            out((2, shard, ni)),
            out((deep, nb)),
            out((8, shard)),
        ),
        in_specs=[away, away] + [here] * 6,
        out_specs=(away,) * 7,
        scratch_shapes=scratch,
        compiler_params=pltpu.CompilerParams(
            collective_id=0, has_side_effects=True, vmem_limit_bytes=VMEM_BYTES
        ),
        name="layer",
    )(patches, cotangent, segments, wq_in, wo_in, wi_in, wb_in, gain_rows)


def adam_step(weight, grad, first, second, rate, shrink):
    first_new = beta_one * first + (1.0 - beta_one) * grad
    second_new = beta_two * second + (1.0 - beta_two) * grad * grad
    first_fix = first_new / (1.0 - beta_one**STEP)
    second_fix = second_new / (1.0 - beta_two**STEP)
    weight_new = weight - rate * (first_fix / (jnp.sqrt(second_fix) + epsilon) + shrink * weight)
    return (first_new, second_new, weight_new)


def update_kernel(*refs):
    inputs, outs, held, news = refs[:22], refs[22:39], refs[39:59], refs[59:74]
    passing, (load_sems, store_sems, pass_sems) = refs[74:76], refs[76:]
    takes = [pltpu.make_async_copy(inputs[i], passing[i], pass_sems.at[i]) for i in range(2)]
    passes = [pltpu.make_async_copy(passing[i], outs[i], pass_sems.at[2 + i]) for i in range(2)]
    loads = [pltpu.make_async_copy(inputs[2 + i], held[i], load_sems.at[i]) for i in range(20)]
    stores = [pltpu.make_async_copy(news[i], outs[2 + i], store_sems.at[i]) for i in range(15)]
    order = (3, 2, 0, 1, 4)
    for at in order:
        for i in (at, 5 + at, 10 + at, 15 + at):
            loads[i].start()
    for copy in takes:
        copy.start()
    gq, go, gi, gb, gg = held[:5]
    state = held[5:]

    def update(at, cols, grad):
        weight, first, second = state[at], state[5 + at], state[10 + at]
        values = adam_step(weight[:, cols], grad, first[:, cols], second[:, cols], rate_list[at], shrink_list[at])
        for to, value in zip(news[3 * at : 3 * at + 3], values):
            to[:, cols] = value

    width = gb.shape[1]
    half = width // 2
    for at in order:
        for i in (at, 5 + at, 10 + at, 15 + at):
            loads[i].wait()
        if at == 0:
            for h in range(2):
                for part in range(3):
                    for p in range(half // 128):
                        grad = gq[p, h, :, pl.ds(part * 128, 128)]
                        update(0, pl.ds(part * width + h * half + p * 128, 128), grad)
        elif at == 1:
            for h in range(2):
                update(1, pl.ds(h * half, half), go[h])
        elif at == 2:
            group = gi.shape[2] // 8
            for pair in range(4):
                cols = pl.ds(2 * pair * group, 2 * group)
                first, second = gi[0, :, cols], gi[1, :, cols]
                low = lanes(first.shape) < group
                update(2, pl.ds(4 * pair * group, 2 * group), jnp.where(low, first, pltpu.roll(second, group, 1)))
                cols = pl.ds((4 * pair + 2) * group, 2 * group)
                update(2, cols, jnp.where(low, pltpu.roll(first, group, 1), second))
        elif at == 3:
            update(3, slice(None), gb[...])
        else:
            update(4, slice(None), gg[0:4, :])
        for i in range(3):
            stores[3 * at + i].start()
        if at == 3:
            for take, copy in zip(takes, passes):
                take.wait()
                copy.start()
    for copy in passes + stores:
        copy.wait()


def update_all(block, patch, grads, state):
    away = pl.BlockSpec(memory_space=pl.ANY)
    like = lambda v: jax.ShapeDtypeStruct(v.shape, v.dtype)
    news = tuple(like(state[i]) for i in range(5) for _ in range(3))
    operands = (*grads, *state)
    return pl.pallas_call(
        update_kernel,
        out_shape=(like(block), like(patch)) + news,
        in_specs=[away] * 22,
        out_specs=(away,) * 17,
        scratch_shapes=[pltpu.VMEM(v.shape, v.dtype) for v in operands]
        + [pltpu.VMEM(v.shape, v.dtype) for v in news]
        + [pltpu.VMEM(v.shape, v.dtype) for v in (block, patch)]
        + [pltpu.SemaphoreType.DMA((n,)) for n in (20, 15, 4)],
        compiler_params=pltpu.CompilerParams(vmem_limit_bytes=VMEM_BYTES),
        name="update",
    )(block, patch, *operands)


def shards(spans, patches, segments, cotangent, *state):
    dp, blk = lax.axis_index("dp"), lax.axis_index("blk")
    index = dp * 2 + blk
    members = 2 * SPAN
    place = index % members
    state = [v.T if i % 5 == 4 else v for i, v in enumerate(state)]
    weights = state[:5]

    def span_rows(weight, axis=0):
        if spans == 1:
            return weight
        whole = lax.all_gather(weight, ("dp", "blk"), axis=axis, tiled=True)
        depth = whole.shape[axis] // members
        return lax.dynamic_slice_in_dim(whole, place * depth, depth, axis)

    def span_sum(grad, rows, axis=0):
        shape = [n * members if i == axis else n for i, n in enumerate(grad.shape)]
        whole = lax.dynamic_update_slice_in_dim(jnp.zeros(shape, f32), grad, place * grad.shape[axis], axis)
        whole = lax.psum(whole, ("dp", "blk"))
        return lax.dynamic_slice_in_dim(whole, index * rows, rows, axis)

    block_out, patch_grad, *grads = run_layer(
        patches[0],
        cotangent[0],
        segments,
        [span_rows(w) for w in weights[:4]],
        span_rows(weights[4], 1),
    )
    if spans > 1:
        rows = [w.shape[0] for w in weights[:4]] + [weights[4].shape[1]]
        grads = [span_sum(g, n, axis) for g, n, axis in zip(grads, rows, (2, 1, 1, 0, 1))]
    block_out, patch_grad, *news = update_all(block_out, patch_grad, grads, state)
    news = [v.T if i >= 12 else v for i, v in enumerate(news)]
    return (block_out[None], patch_grad[None], *news)


def solution(mesh):
    rows, tokens = P(("dp", "blk"), None), P("dp", "blk", None)
    return jax.shard_map(
        functools.partial(shards, mesh.shape["dp"] // SPAN),
        mesh=mesh,
        in_specs=(tokens, P("dp", None), tokens) + (rows,) * 15,
        out_specs=(tokens, tokens) + (rows,) * 15,
        check_vma=False,
    )
```
